512 devices in a mesh: visit: 8 (over x, y_hi), patch: 64 (over z, y_lo, core).
Axes of the slice: x: 4, y: 4 (y_hi: 2, y_lo: 2; y = y_hi * 2 + y_lo), z: 16, core: 2. Of those that a mesh axis runs over, the one named last changes fastest.
Arguments:
- images: bfloat16 [8, 2048, 128, 128], P('visit', 'patch'), may hold values from -6 to 6
- intersection: int32 [8, 2048, 2], P('visit', 'patch'), may hold values from 0 to 63, all different within a row; in each aligned block of 32 rows (0 to 31, 32 to 63, ..., all dimensions but the last counted through in order) at most 2 rows name the same one
- offsets: int32 [8, 2048, 2, 2], P('visit', 'patch'), may hold values from 0 to 127
- subpixel: bfloat16 [8, 2048, 2, 2], P('visit', 'patch'), may hold values from 0 to 1
- variance: bfloat16 [8, 2048], P('visit', 'patch'), may hold values from 0.099609375 to 10
- basis_index: int32 [8, 2048], P('visit', 'patch'), may hold values from 0 to 63
- coefficients: float32 [64, 3, 3], replicated, may hold values from -4 to 4
Outputs:
- significance: float32 [64, 256, 256], P('patch', 'visit')
The draws below stay inside these ranges and needn't reach their ends.
Inputs may be any that keep to these rules, and one draw needn't show every extreme that they name: `intersection`: each cell's 2 entries are different patches; among the 32 cells held by one device no patch is named more than 2 times, and in every draw some device's cells name some patch exactly 2 times.
All inputs are finite; a program needn't handle non-finite values.
Results may differ from the reference program's by a relative error of at most 0.0053.
Values may be sent and summed in bfloat16 or wider, within the bound.
A program may use at most 64 MiB of HBM per device.

```python
import math
import jax
import jax.numpy as jnp
import numpy as np
from jax import lax

PIX = 128
PPIX = 256
NB = 3
TOP = 2
SETS = 64
BLK_DEV = 32
BLOCKS = 2048
PATCHES = 64
CAP = 2
N_VISIT = 8


def with_ends(result, own_key, low, top_value):
    index_at = [jax.random.randint(jax.random.fold_in(own_key, axis), (), 0, length) for axis, length in enumerate(result.shape)]
    widest = result.shape.index(max(result.shape))
    next_to = index_at[:widest] + [(index_at[widest] + 1) % result.shape[widest]] + index_at[widest + 1:]
    return result.at[tuple(index_at)].set(low).at[tuple(next_to)].set(top_value)


def block_scale(key, extent, split, least, high):
    factor_of, own = 1.0, jax.random.fold_in(key, 6)
    for axis_at, shards_of in split:
        draws = jnp.exp(jax.random.uniform(jax.random.fold_in(own, axis_at), (shards_of,), jnp.float32, least / len(split), high / len(split)))
        factor_of = factor_of * jnp.repeat(draws, extent[axis_at] // shards_of).reshape([-1 if axis == axis_at else 1 for axis in range(len(extent))])
    return factor_of


def shared_out(stream_key, own, number, rows, count, top, most, skew):
    sequence = jax.random.permutation(stream_key, count)
    heavy_load, usual = portions_of(count, rows * top, most, skew, True), portions_of(count, rows * top, most, skew, False)
    places = jnp.arange(count)

    def named(lengths, rotation):
        used = int((lengths > 0).sum())
        fixed = max(1, used // 4)
        passed = fixed + (places - fixed + rotation * (used - fixed)) % max(1, count - fixed)
        return jnp.zeros((count,), jnp.int32).at[sequence[jnp.where(places < fixed, places, passed)]].set(jnp.asarray(lengths, jnp.int32))

    lengths = jnp.where(number % 4 == 0, named(heavy_load, number // 4), named(usual, number - number // 4 - 1))
    mixed = jax.random.permutation(jax.random.fold_in(own, 3), count)
    donor, sink = mixed[0:count // 2 * 2:2], mixed[1:count // 2 * 2:2]
    margin = jnp.minimum(lengths[donor] - 1, most - lengths[sink]) // 2
    margin = jnp.where((donor == sequence[0]) | (sink == sequence[0]) | (lengths[sink] == 0), 0, jnp.maximum(margin, 0))
    passed = jax.random.randint(jax.random.fold_in(own, 4), (count // 2,), 0, 1 << 20) % (margin + 1)
    lengths = lengths.at[donor].add(-passed).at[sink].add(passed)
    items = jnp.searchsorted(jnp.cumsum(lengths), jnp.arange(rows * top), side="right").astype(jnp.int32)
    table = items.reshape(top, rows).T
    table = table[jax.random.permutation(jax.random.fold_in(own, 1), rows)]
    rotation = jax.random.randint(jax.random.fold_in(own, 2), (rows, 1), 0, top)
    return jnp.take_along_axis(table, (jnp.arange(top)[None, :] + rotation) % top, axis=1)


def portions_of(count, total, limit, slope, full):
    loads = [(1 << 20) // math.isqrt(grade ** slope) + 1 for grade in range(1, count + 1)]
    largest = limit if full else min(limit, max(-(-total // count), total * loads[0] // sum(loads)))
    least = 1 if total - largest >= count - 1 else 0
    counts, rest = [largest] + [least] * (count - 1), total - largest - least * (count - 1)
    while rest > 0:
        free = [i for i in range(1, count) if counts[i] < largest] or [i for i in range(1, count) if counts[i] < limit]
        whole, remaining = sum([loads[i] for i in free]), rest
        for i in free:
            addition = min(limit - counts[i], max(1, remaining * loads[i] // whole), rest)
            counts[i] = counts[i] + addition
            rest = rest - addition
    return np.array(counts)


def scatter_about(key, extent, deviation, bound, split=(), held_as=jnp.bfloat16):
    factor_of = block_scale(key, extent, split, -0.22, 0.18) if split else 1.0
    array = jax.random.normal(key, extent, jnp.float32) * deviation * factor_of
    return jnp.minimum(jnp.maximum(array, -bound), bound).astype(held_as)


def setup_inputs(seed: int = 0) -> dict:
    keys = jax.random.split(jax.random.key(seed), 8)
    images = scatter_about(keys[0], (N_VISIT, BLOCKS, PIX, PIX), 1.0, 6.0, ((0, 8), (1, 64)))
    intersection_keys = jax.random.split(jax.random.fold_in(keys[1], 1), N_VISIT * BLOCKS // BLK_DEV)
    intersection_turns = jax.random.permutation(jax.random.fold_in(keys[1], 3), N_VISIT * BLOCKS // BLK_DEV)
    intersection = jax.vmap(lambda own, number: shared_out(jax.random.fold_in(keys[1], 2), own, number, BLK_DEV, PATCHES, TOP, CAP, 2))(intersection_keys, intersection_turns).reshape((N_VISIT, BLOCKS, TOP))
    offsets = with_ends(jax.random.randint(keys[2], (N_VISIT, BLOCKS, TOP, 2), 0, PPIX - PIX), jax.random.fold_in(keys[2], 1), 0, (PPIX - PIX) - 1).astype(jnp.int32)
    subpixel = jnp.clip(1.0 * jax.random.uniform(keys[3], (N_VISIT, BLOCKS, TOP, 2), jnp.float32) ** block_scale(keys[3], (N_VISIT, BLOCKS, TOP, 2), ((0, 8), (1, 64)), -0.2, 0.2), 0.0, 1.0).astype(jnp.bfloat16)
    variance = jnp.clip(jnp.exp(math.log(10.0) - 4.609084 * jax.random.uniform(keys[4], (N_VISIT, BLOCKS), jnp.float32) ** block_scale(keys[4], (N_VISIT, BLOCKS), ((0, 8), (1, 64)), -0.2, 0.2)), 0.099609375, 10.0).astype(jnp.bfloat16)
    basis_index = with_ends(jax.random.randint(keys[5], (N_VISIT, BLOCKS), 0, SETS), jax.random.fold_in(keys[5], 1), 0, SETS - 1).astype(jnp.int32)
    coefficients = scatter_about(keys[6], (SETS, NB, 3), 1.0, 4.0, (), jnp.float32)
    return dict(images=images, intersection=intersection, offsets=offsets, subpixel=subpixel, variance=variance, basis_index=basis_index, coefficients=coefficients)


def kernel_tables(block_side):
    places = jnp.arange(block_side, dtype=jnp.float32)
    spread = places[:, None] - places[None, :]
    widths = 2.0 ** jnp.arange(NB, dtype=jnp.float32)
    profile = jnp.exp(-spread[None] ** 2 / (2.0 * widths[:, None, None] ** 2))
    return (profile / (math.sqrt(2.0 * math.pi) * widths[:, None, None])).astype(jnp.bfloat16)

def match_blocks(blocks_in, mixing, kernels):
    how_many = blocks_in.shape[0]
    block_side = blocks_in.shape[-1]
    stacked = jnp.transpose(kernels, (2, 0, 1)).reshape(block_side, NB * block_side)
    rows_done = jnp.einsum('nia,ab->nib', blocks_in.astype(jnp.float32), stacked.astype(jnp.float32)).astype(jnp.bfloat16)
    rows_done = rows_done.reshape(how_many, block_side, NB, block_side)
    smoothed = jnp.einsum('kia,nakj->nkij', kernels.astype(jnp.float32), rows_done.astype(jnp.float32))
    ramp_axis = (2.0 * jnp.arange(block_side, dtype=jnp.float32) - (block_side - 1)) / (block_side - 1)
    mix_map = mixing[:, :, 0, None, None] + mixing[:, :, 1, None, None] * ramp_axis[None, None, :, None] + mixing[:, :, 2, None, None] * ramp_axis[None, None, None, :]
    return lax.optimization_barrier(jnp.sum(mix_map * smoothed, axis=1)).astype(jnp.bfloat16)

def placement(offset, fraction, out_rows, block_side):
    out_index = jnp.arange(out_rows, dtype=jnp.int32)[None, :, None]
    in_index = jnp.arange(block_side, dtype=jnp.int32)[None, None, :]
    distance = out_index - in_index - offset.astype(jnp.int32)[:, None, None]
    share = fraction[:, None, None]
    return (jnp.where(distance == 0, 1.0 - share, 0.0) + jnp.where(distance == 1, share, 0.0)).astype(jnp.bfloat16)

def reference(images, intersection, offsets, subpixel, variance, basis_index, coefficients):
    block_total = N_VISIT * BLOCKS
    batch_size = math.gcd(block_total, 64)
    turn_count = block_total // batch_size
    kernels = kernel_tables(PIX)
    packed = (images.reshape(turn_count, batch_size, PIX, PIX), intersection.reshape(turn_count, batch_size * TOP), offsets.reshape(turn_count, batch_size * TOP, 2), subpixel.reshape(turn_count, batch_size * TOP, 2), variance.reshape(turn_count, batch_size), basis_index.reshape(turn_count, batch_size))

    def accumulate(totals, batch_in):
        numerator, weight = totals
        blocks_in, targets, shifts, fractions, variances, set_ids = batch_in
        matched = match_blocks(blocks_in, coefficients[set_ids], kernels)
        inverse_var = jnp.repeat(1.0 / variances.astype(jnp.float32), TOP)
        matched_rows = jnp.repeat(matched, TOP, axis=0)
        fractions = fractions.astype(jnp.float32)
        down_place = placement(shifts[:, 0], fractions[:, 0], PPIX, PIX)
        across = placement(shifts[:, 1], fractions[:, 1], PPIX, PIX)
        placed = jnp.einsum('sij,skj->sik', matched_rows.astype(jnp.float32), across.astype(jnp.float32))
        placed = (inverse_var[:, None, None] * placed).astype(jnp.bfloat16)
        contribution = jnp.einsum('sij,sjk->sik', down_place.astype(jnp.float32), placed.astype(jnp.float32))
        down_sum = lax.optimization_barrier(jnp.sum(down_place.astype(jnp.float32), axis=2))
        across_sum = lax.optimization_barrier(jnp.sum(across.astype(jnp.float32), axis=2))
        coverage = (inverse_var[:, None] * down_sum)[:, :, None] * across_sum[:, None, :]
        numerator = numerator.at[targets].add(contribution)
        weight = weight.at[targets].add(coverage)
        return ((numerator, weight), None)
    start_totals = (jnp.zeros((PATCHES, PPIX, PPIX), jnp.float32), jnp.zeros((PATCHES, PPIX, PPIX), jnp.float32))
    (numerator, weight), _ = lax.scan(accumulate, start_totals, packed)
    return numerator / jnp.sqrt(weight + 1.0)
```

```python
import math

import jax
import jax.numpy as jnp
from jax import lax
from jax.experimental import pallas as pl
from jax.experimental.pallas import tpu as pltpu
from jax.sharding import PartitionSpec as P

PIX = 128
PPIX = 256
NB = 3
CELLS = 32
PAIRS = 64
PATCHES = 64
DEPTH = 16
PARTS = 4
ROWS = 32
F32, BF16, I32 = jnp.float32, jnp.bfloat16, jnp.int32
MESH = pl.DeviceIdType.MESH
VMEM_LIMIT = 56 * 1024 * 1024


def distance_at(k):
    if isinstance(k, int):
        return 8 + k // 2 if k % 2 == 0 else 7 - k // 2
    return jnp.where(k % 2 == 0, 8 + k // 2, 7 - k // 2)


def position():
    v, p = lax.axis_index("visit"), lax.axis_index("patch")
    return v // 2, (v % 2) * 2 + (p // 2) % 2, p // 4, p % 2


def device_at(x, y, z, c):
    return {"visit": x * 2 + y // 2, "patch": z * 4 + (y % 2) * 2 + c}


def iota(shape, axis):
    return lax.broadcasted_iota(I32, shape, axis)


def local_kernel(
    inter, offs, frac, inv, basis, coef, images, target_row, target_col, fields,
    tiles, meta, matched, table, count,
):
    x, y, z, c = position()

    @pl.loop(0, PATCHES)
    def _(i):
        count[i] = 0
        table[2 * i] = -1
        table[2 * i + 1] = -1

    @pl.loop(0, PAIRS)
    def _(s):
        p = inter[s]
        rank = count[p]
        table[2 * p + rank] = s
        count[p] = rank + 1

    spread = (iota((PIX, PIX), 0) - iota((PIX, PIX), 1)).astype(F32)
    kernels = []
    for k in range(NB):
        width = 2.0**k
        profile = jnp.exp(-(spread**2) / (2.0 * width**2))
        kernels.append((profile / (math.sqrt(2.0 * math.pi) * width)).astype(BF16))
    stacked = jnp.concatenate(kernels, axis=1)
    ramp_i = (2.0 * iota((PIX, PIX), 0).astype(F32) - (PIX - 1)) / (PIX - 1)
    ramp_j = (2.0 * iota((PIX, PIX), 1).astype(F32) - (PIX - 1)) / (PIX - 1)

    @pl.loop(0, CELLS // 2)
    def _(g):
        rows = jnp.dot(
            images[pl.ds(2 * g, 2)].reshape(2 * PIX, PIX), stacked, preferred_element_type=F32
        ).astype(BF16)
        total = [None, None]
        for k in range(NB):
            part = rows[:, k * PIX : (k + 1) * PIX]
            wide = jnp.concatenate([part[:PIX], part[PIX:]], axis=1)
            smooth = jnp.dot(kernels[k], wide, preferred_element_type=F32)
            for b in range(2):
                at = basis[2 * g + b] * (NB * 3) + 3 * k
                mix = coef[at] + coef[at + 1] * ramp_i + coef[at + 2] * ramp_j
                term = mix * smooth[:, b * PIX : (b + 1) * PIX]
                total[b] = term if k == 0 else total[b] + term
        for b in range(2):
            matched[2 * g + b] = total[b].astype(BF16)

    across_at = iota((PIX, PPIX), 1) - iota((PIX, PPIX), 0)
    down_at = iota((PPIX, PIX), 0) - iota((PPIX, PIX), 1)

    def one_hot(at, offset, share):
        return jnp.where(
            at == offset, 1.0 - share, jnp.where(at == offset + 1, share, 0.0)
        ).astype(BF16)

    @pl.loop(0, DEPTH)
    def _(k):
        z_to = lax.rem(z + distance_at(k), DEPTH)
        for r in range(2):
            for y_lo in range(2):
                p = z_to * 4 + y_lo * 2 + (c if r == 0 else 1 - c)
                downs, placed = [], []
                for slot in range(2):
                    s = table[2 * p + slot]
                    filled = s >= 0
                    s = jnp.maximum(s, 0)
                    scale = jnp.where(filled, inv[s // 2], 0.0)
                    across = one_hot(across_at, offs[2 * s + 1], frac[2 * s + 1])
                    wide = jnp.dot(matched[s // 2], across, preferred_element_type=F32)
                    placed.append((scale * wide).astype(BF16))
                    downs.append(one_hot(down_at, offs[2 * s], frac[2 * s]))
                tile = jnp.dot(
                    jnp.concatenate(downs, axis=1),
                    jnp.concatenate(placed, axis=0),
                    preferred_element_type=F32,
                ).astype(BF16)
                for x_to in range(4):
                    for y_hi in range(2):
                        at = (x_to * 2 + y_hi) * ROWS
                        y_to = y_hi * 2 + y_lo
                        block = tile[at : at + ROWS]
                        tiles[r, k // 4, 0, x_to, k % 4, y_to] = block[:, :PIX]
                        tiles[r, k // 4, 1, y_to, k % 4, x_to] = block[:, PIX:]

    same = target_col[...] == target_row[...]
    earlier = iota((PAIRS, PAIRS), 1) < iota((PAIRS, PAIRS), 0)
    rank = jnp.sum(jnp.where(same & earlier, 1, 0), axis=1, keepdims=True)
    code = 2 * target_col[...] + rank
    lane = iota((PAIRS, PIX), 1)
    mine = lane // 8 == z
    for k in range(DEPTH):
        z_to = lax.rem(z + distance_at(k), DEPTH)
        pick = jnp.where((code == z_to * 8 + lane % 8) & mine, 1.0, 0.0).astype(BF16)
        meta[k] = jnp.dot(fields[...], pick, preferred_element_type=F32)


class Copies:
    def __init__(self, send, recv):
        self.send, self.recv, self.used = send, recv, 0

    def new(self, src, dst, device):
        at = self.used
        self.used += 1
        return pltpu.make_async_remote_copy(
            src_ref=src,
            dst_ref=dst,
            send_sem=self.send.at[at],
            recv_sem=self.recv.at[at],
            device_id=device,
            device_id_type=MESH,
        )


def add_into(dst, src):
    dst[...] = (dst[...].astype(F32) + src[...].astype(F32)).astype(BF16)


class Ring:
    def __init__(self, copies, me, device, blocks, relay, fin):
        half = blocks.shape[1] // 2
        lo, hi = pl.ds(0, half), pl.ds(half, half)
        right, left, far = (me + 1) % 4, (me + 3) % 4, (me + 2) % 4
        to_right, to_left = device(right), device(left)
        self.blocks, self.relay, self.fin = blocks, relay, fin
        self.me, self.left, self.right, self.lo, self.hi = me, left, right, lo, hi
        self.first = [
            copies.new(blocks.at[far, lo], relay.at[0], to_right),
            copies.new(blocks.at[far, hi], relay.at[1], to_left),
            copies.new(blocks.at[right, hi], fin.at[0, hi], to_right),
            copies.new(blocks.at[left, lo], fin.at[1, lo], to_left),
        ]
        self.second = [
            copies.new(blocks.at[right, lo], fin.at[0, lo], to_right),
            copies.new(blocks.at[left, hi], fin.at[1, hi], to_left),
        ]

    def start(self):
        for copy in self.first:
            copy.start()

    def forward(self):
        self.first[0].wait_recv()
        add_into(self.blocks.at[self.right, self.lo], self.relay.at[0])
        self.second[0].start()
        self.first[1].wait_recv()
        add_into(self.blocks.at[self.left, self.hi], self.relay.at[1])
        self.second[1].start()

    def finish(self):
        for copy in self.first[2:] + self.second:
            copy.wait_recv()

    def result(self, i):
        own = self.blocks[self.me, i].astype(F32)
        return own + self.fin[0, i].astype(F32) + self.fin[1, i].astype(F32)

    def drain(self):
        for copy in self.first + self.second:
            copy.wait_send()


def share_kernel(
    tiles, meta, out,
    core_in, relay1, fin1, blocks2, relay2, fin2, blocks3, far_in,
    meta_z, meta_x, meta_y, meta_c, send_sem, recv_sem,
):
    x, y, z, c = position()
    peers = [device_at(x, y, z, 1 - c)]
    peers += [device_at((x + d) % 4, y, z, c) for d in (1, 2, 3)]
    peers += [device_at(x, (y + d) % 4, z, c) for d in (1, 2, 3)]
    peers += [device_at(x, y, (z + d) % DEPTH, c) for d in range(1, DEPTH)]
    barrier = pltpu.get_barrier_semaphore()
    for peer in peers:
        pl.semaphore_signal(barrier, inc=1, device_id=peer, device_id_type=MESH)
    pl.semaphore_wait(barrier, len(peers))

    copies = Copies(send_sem, recv_sem)
    x_device = lambda to: device_at(to, y, z, c)
    y_device = lambda to: device_at(x, to, z, c)
    z_device = lambda k: device_at(x, y, (z + distance_at(k)) % DEPTH, c)

    core = [
        copies.new(tiles.at[1, q], core_in.at[q], device_at(x, y, z, 1 - c)) for q in range(PARTS)
    ]
    for copy in core:
        copy.start()

    meta_copies = [copies.new(meta.at[k], meta_z.at[k], z_device(k)) for k in range(DEPTH - 1)]
    for copy in meta_copies:
        copy.start()
    meta_z[DEPTH - 1] = meta[DEPTH - 1]

    rings1, rings2, sent3 = {}, {}, []

    def enter(q):
        core[q].wait_recv()

        for half in range(2):
            @pl.loop(0, 4)
            def _(i, half=half):
                add_into(core_in.at[q, half, i], tiles.at[0, q, half, i])

        for half in range(2):
            me, device = ((x, x_device), (y, y_device))[half]
            rings1[q, half] = Ring(
                copies, me, device, core_in.at[q, half], relay1.at[q, half], fin1.at[q, half]
            )
            rings1[q, half].start()

    def middle(q):
        for half in range(2):
            rings1[q, half].forward()

    def turn(q):
        for half in range(2):
            ring = rings1[q, half]
            ring.finish()
            for i in range(4):
                block = ring.result(i).astype(BF16)
                for other in range(4):
                    blocks2[q, half, other, i] = block[other]
            me, device = ((y, y_device), (x, x_device))[half]
            rings2[q, half] = Ring(
                copies, me, device, blocks2.at[q, half], relay2.at[q, half], fin2.at[q, half]
            )
            rings2[q, half].start()

    def middle2(q):
        for half in range(2):
            rings2[q, half].forward()

    def leave(q):
        for half in range(2):
            ring = rings2[q, half]
            ring.finish()
            for i in range(4):
                k = 4 * q + i
                if k < DEPTH - 1:
                    blocks3[k, half] = ring.result(i).astype(BF16)
                else:
                    far_in[k, half] = ring.result(i).astype(BF16)
        for i in range(4):
            k = 4 * q + i
            if k < DEPTH - 1:
                copy = copies.new(blocks3.at[k], far_in.at[k], z_device(k))
                copy.start()
                sent3.append(copy)

    def meta_plane():
        for copy in meta_copies:
            copy.wait_recv()
        total = meta_z[0]
        for k in range(1, DEPTH):
            total = total + meta_z[k]
        meta_x[x] = total
        sent = []
        for d in (1, 2, 3):
            sent.append(copies.new(meta_x.at[x], meta_x.at[x], x_device((x + d) % 4)))
        for copy in sent:
            copy.start()
        meta_copies.extend(sent)
        return sent

    def meta_second(before):
        for copy in before:
            copy.wait_recv()
        meta_y[y] = meta_x[...]
        sent = []
        for d in (1, 2, 3):
            sent.append(copies.new(meta_y.at[y], meta_y.at[y], y_device((y + d) % 4)))
        for copy in sent:
            copy.start()
        meta_copies.extend(sent)
        return sent

    def meta_third(before):
        for copy in before:
            copy.wait_recv()
        copy = copies.new(meta_y, meta_c, device_at(x, y, z, 1 - c))
        copy.start()
        meta_copies.append(copy)
        return copy

    enter(0)
    enter(1)
    middle(0)
    sent_x = meta_plane()
    enter(2)
    turn(0)
    middle(1)
    sent_y = meta_second(sent_x)
    enter(3)
    middle2(0)
    turn(1)
    middle(2)
    sent_c = meta_third(sent_y)
    leave(0)
    middle2(1)
    turn(2)
    middle(3)
    leave(1)
    middle2(2)
    turn(3)
    leave(2)
    middle2(3)

    sent_c.wait_recv()
    combo = (y % 2) * 2 + c
    lane = iota((8, PIX), 1)
    mine = (lane // 2) % 4 == combo
    row_at = (iota((ROWS, PIX), 0) + (x * 2 + y // 2) * ROWS).astype(F32)
    column_at = iota((PPIX, PIX), 0).astype(F32)

    def cover(at, offset, share):
        rest = (1.0 - share).astype(BF16).astype(F32)
        d = at - offset
        first = jnp.where((d >= 0.0) & (d < float(PIX)), rest, 0.0)
        return first + jnp.where((d >= 1.0) & (d < float(PIX + 1)), share, 0.0)

    weight = jnp.zeros((ROWS, PPIX), F32)
    for source in (meta_y, meta_c):
        for b in range(4):
            full = jnp.zeros((8, PIX), F32)
            for m in range(4):
                kept = jnp.where(mine, source[b, m], 0.0)
                full = full + pltpu.roll(kept, (2 * (m - combo)) % PIX, 1)
            valid = full[5:6] > 0.0
            inverse = jnp.where(valid, 1.0 / jnp.where(valid, full[4:5], 1.0), 0.0)
            down = inverse * cover(row_at, full[0:1], full[2:3])
            across = cover(column_at, full[1:2], full[3:4])
            weight = weight + lax.dot_general(
                down, across, (((1,), (1,)), ((), ())),
                precision=lax.Precision.HIGHEST, preferred_element_type=F32,
            )

    leave(3)
    for copy in sent3:
        copy.wait_recv()
    for half in range(2):
        total = far_in[0, half].astype(F32)
        for k in range(1, DEPTH):
            total = total + far_in[k, half].astype(F32)
        across = slice(half * PIX, (half + 1) * PIX)
        out[:, across] = total / jnp.sqrt(weight[:, across] + 1.0)

    for copy in core + meta_copies + sent3:
        copy.wait_send()
    for ring in list(rings1.values()) + list(rings2.values()):
        ring.drain()


COPY_COUNT = PARTS + PARTS * 24 + (DEPTH - 1) * 2 + 7


def body(images, intersection, offsets, subpixel, variance, basis_index, coefficients):
    target = intersection[0].reshape(PAIRS)
    shifts = offsets[0].reshape(PAIRS, 2)
    shares = subpixel[0].reshape(PAIRS, 2).astype(F32)
    inverse = 1.0 / variance[0].astype(F32)
    spare = jnp.zeros((PAIRS,), BF16)
    fields = jnp.stack(
        [
            shifts[:, 0].astype(BF16),
            shifts[:, 1].astype(BF16),
            subpixel[0].reshape(PAIRS, 2)[:, 0],
            subpixel[0].reshape(PAIRS, 2)[:, 1],
            jnp.repeat(variance[0], 2),
            spare + 1,
            spare,
            spare,
        ]
    )
    smem = pl.BlockSpec(memory_space=pltpu.SMEM)
    vmem = pl.BlockSpec(memory_space=pltpu.VMEM)
    tiles, meta = pl.pallas_call(
        local_kernel,
        out_shape=(
            jax.ShapeDtypeStruct((2, PARTS, 2, 4, 4, 4, ROWS, PIX), BF16),
            jax.ShapeDtypeStruct((DEPTH, 8, PIX), F32),
        ),
        in_specs=[smem] * 6 + [vmem] * 4,
        out_specs=(vmem, vmem),
        scratch_shapes=[
            pltpu.VMEM((CELLS, PIX, PIX), BF16),
            pltpu.SMEM((2 * PATCHES,), I32),
            pltpu.SMEM((PATCHES,), I32),
        ],
        compiler_params=pltpu.CompilerParams(vmem_limit_bytes=VMEM_LIMIT),
    )(
        target,
        shifts.reshape(2 * PAIRS),
        shares.reshape(2 * PAIRS),
        inverse,
        basis_index[0],
        coefficients.reshape(-1),
        images[0],
        target.reshape(1, PAIRS),
        target.reshape(PAIRS, 1),
        fields,
    )
    out = pl.pallas_call(
        share_kernel,
        out_shape=jax.ShapeDtypeStruct((ROWS, PPIX), F32),
        in_specs=[vmem] * 2,
        out_specs=vmem,
        scratch_shapes=[
            pltpu.VMEM((PARTS, 2, 4, 4, 4, ROWS, PIX), BF16),
            pltpu.VMEM((PARTS, 2, 2, 2, 4, ROWS, PIX), BF16),
            pltpu.VMEM((PARTS, 2, 2, 4, 4, ROWS, PIX), BF16),
            pltpu.VMEM((PARTS, 2, 4, 4, ROWS, PIX), BF16),
            pltpu.VMEM((PARTS, 2, 2, 2, ROWS, PIX), BF16),
            pltpu.VMEM((PARTS, 2, 2, 4, ROWS, PIX), BF16),
            pltpu.VMEM((DEPTH - 1, 2, ROWS, PIX), BF16),
            pltpu.VMEM((DEPTH, 2, ROWS, PIX), BF16),
            pltpu.VMEM((DEPTH, 8, PIX), F32),
            pltpu.VMEM((4, 8, PIX), F32),
            pltpu.VMEM((4, 4, 8, PIX), F32),
            pltpu.VMEM((4, 4, 8, PIX), F32),
            pltpu.SemaphoreType.DMA((COPY_COUNT,)),
            pltpu.SemaphoreType.DMA((COPY_COUNT,)),
        ],
        compiler_params=pltpu.CompilerParams(
            collective_id=0, has_side_effects=True, vmem_limit_bytes=VMEM_LIMIT
        ),
    )(tiles, meta)
    return out[None]


def solution(mesh):
    return jax.shard_map(
        body,
        mesh=mesh,
        in_specs=(
            P("visit", "patch", None, None),
            P("visit", "patch", None),
            P("visit", "patch", None, None),
            P("visit", "patch", None, None),
            P("visit", "patch"),
            P("visit", "patch"),
            P(),
        ),
        out_specs=P("patch", "visit", None),
        check_vma=False,
    )
```

```python
import math

import jax
import jax.numpy as jnp
from jax import lax
from jax.experimental import pallas as pl
from jax.experimental.pallas import tpu as pltpu
from jax.sharding import PartitionSpec as P

PIX = 128
PPIX = 256
NB = 3
CELLS = 32
PAIRS = 64
PATCHES = 64
DEPTH = 16
PARTS = 4
ROWS = 32
F32, BF16, I32 = jnp.float32, jnp.bfloat16, jnp.int32
MESH = pl.DeviceIdType.MESH
GROUP = 8
VMEM_LIMIT = 56 * 1024 * 1024


def distance_at(k):
    if isinstance(k, int):
        return 8 + k // 2 if k % 2 == 0 else 7 - k // 2
    return jnp.where(k % 2 == 0, 8 + k // 2, 7 - k // 2)


def position():
    v, p = lax.axis_index("visit"), lax.axis_index("patch")
    return v // 2, (v % 2) * 2 + (p // 2) % 2, p // 4, p % 2


def device_at(x, y, z, c):
    return {"visit": x * 2 + y // 2, "patch": z * 4 + (y % 2) * 2 + c}


def iota(shape, axis):
    return lax.broadcasted_iota(I32, shape, axis)


def match_kernel(
    inter, offs, basis, coef, images, inter_v, offs_v, frac_v, var_v,
    matched, table, shares, meta, shares_v, count, sem,
):
    z = position()[2]
    for t in range(2):
        for axis in range(2):
            shares_v[2 * t + axis : 2 * t + axis + 1, :CELLS] = frac_v[t, axis : axis + 1].astype(F32)
    shares_v[4:5, :CELLS] = 1.0 / var_v[...].astype(F32)
    move = pltpu.make_async_copy(shares_v, shares, sem)
    move.start()

    @pl.loop(0, PATCHES, unroll=8)
    def _(i):
        count[i] = 0
        table[2 * i] = -1
        table[2 * i + 1] = -1

    spread = (iota((PIX, PIX), 0) - iota((PIX, PIX), 1)).astype(F32)
    kernels = []
    for k in range(NB):
        width = 2.0**k
        profile = jnp.exp(-(spread**2) / (2.0 * width**2))
        kernels.append((profile / (math.sqrt(2.0 * math.pi) * width)).astype(BF16))
    stacked = jnp.concatenate(kernels, axis=1)
    ramp_i = (2.0 * iota((PIX, PIX), 0).astype(F32) - (PIX - 1)) / (PIX - 1)
    ramp_j = (2.0 * iota((PIX, PIX), 1).astype(F32) - (PIX - 1)) / (PIX - 1)

    @pl.loop(0, CELLS // GROUP)
    def _(g):
        for b in range(GROUP):
            for t in range(2):
                p = inter[t, GROUP * g + b]
                rank = count[p]
                table[2 * p + rank] = 2 * (GROUP * g + b) + t
                count[p] = rank + 1
        rows = jnp.dot(
            images[pl.ds(GROUP * g, GROUP)].reshape(GROUP * PIX, PIX),
            stacked,
            preferred_element_type=F32,
        ).astype(BF16)
        total = [None] * GROUP
        for k in range(NB):
            part = rows[:, k * PIX : (k + 1) * PIX]
            wide = jnp.concatenate([part[b * PIX : (b + 1) * PIX] for b in range(GROUP)], axis=1)
            smooth = jnp.dot(kernels[k], wide, preferred_element_type=F32)
            for b in range(GROUP):
                q = basis[0, GROUP * g + b]
                mix = coef[k, 0, q] + coef[k, 1, q] * ramp_i + coef[k, 2, q] * ramp_j
                term = mix * smooth[:, b * PIX : (b + 1) * PIX]
                total[b] = term if k == 0 else total[b] + term
        for b in range(GROUP):
            matched[GROUP * g + b] = total[b].astype(BF16)

    target = inter_v[...].astype(F32)
    eye = (iota((CELLS, CELLS), 0) == iota((CELLS, CELLS), 1)).astype(F32).astype(BF16)
    column = lax.dot_general(
        eye, target.astype(BF16), (((1,), (1,)), ((), ())), preferred_element_type=F32
    )
    earlier = iota((CELLS, CELLS), 1) < iota((CELLS, CELLS), 0)
    lane = iota((CELLS, PIX), 1)
    mine = lane // 8 == z
    place = (lane % 8).astype(F32)
    codes, fields = [], []
    for t in range(2):
        rank = jnp.zeros((CELLS, 1), F32)
        for other in range(2):
            same = (column[:, t : t + 1] == target[other : other + 1]) & earlier
            rank = rank + jnp.sum(jnp.where(same, 1.0, 0.0), axis=1, keepdims=True)
        codes.append(2.0 * column[:, t : t + 1] + rank)
        row = iota((8, CELLS), 0)
        field = jnp.where(row == 0, offs_v[t, 0:1].astype(F32), 0.0)
        field = jnp.where(row == 1, offs_v[t, 1:2].astype(F32), field)
        field = jnp.where(row == 2, frac_v[t, 0:1].astype(F32), field)
        field = jnp.where(row == 3, frac_v[t, 1:2].astype(F32), field)
        field = jnp.where(row == 4, var_v[...].astype(F32), field)
        fields.append(jnp.where(row == 5, 1.0, field).astype(BF16))
    for k in range(DEPTH):
        z_to = lax.rem(z + distance_at(k), DEPTH)
        total = jnp.zeros((8, PIX), F32)
        for t in range(2):
            chosen = (codes[t] == (z_to * 8).astype(F32) + place) & mine
            pick = jnp.where(chosen, 1.0, 0.0).astype(BF16)
            total = total + jnp.dot(fields[t], pick, preferred_element_type=F32)
        meta[k] = total
    move.wait()


class Copies:
    def __init__(self, send, recv):
        self.send, self.recv, self.used = send, recv, 0

    def new(self, src, dst, device):
        at = self.used
        self.used += 1
        return pltpu.make_async_remote_copy(
            src_ref=src,
            dst_ref=dst,
            send_sem=self.send.at[at],
            recv_sem=self.recv.at[at],
            device_id=device,
            device_id_type=MESH,
        )


def add_into(dst, src):
    dst[...] = (dst[...].astype(F32) + src[...].astype(F32)).astype(BF16)


class Ring:
    def __init__(self, copies, me, device, blocks, relay, fin):
        half = blocks.shape[1] // 2
        lo, hi = pl.ds(0, half), pl.ds(half, half)
        right, left, far = (me + 1) % 4, (me + 3) % 4, (me + 2) % 4
        to_right, to_left = device(right), device(left)
        self.blocks, self.relay, self.fin = blocks, relay, fin
        self.me, self.left, self.right, self.lo, self.hi = me, left, right, lo, hi
        self.first = [
            copies.new(blocks.at[far, lo], relay.at[0], to_right),
            copies.new(blocks.at[far, hi], relay.at[1], to_left),
            copies.new(blocks.at[right, hi], fin.at[0, hi], to_right),
            copies.new(blocks.at[left, lo], fin.at[1, lo], to_left),
        ]
        self.second = [
            copies.new(blocks.at[right, lo], fin.at[0, lo], to_right),
            copies.new(blocks.at[left, hi], fin.at[1, hi], to_left),
        ]

    def start(self):
        for copy in self.first:
            copy.start()

    def forward(self):
        self.first[0].wait_recv()
        add_into(self.blocks.at[self.right, self.lo], self.relay.at[0])
        self.second[0].start()
        self.first[1].wait_recv()
        add_into(self.blocks.at[self.left, self.hi], self.relay.at[1])
        self.second[1].start()

    def finish(self):
        for copy in self.first[2:] + self.second:
            copy.wait_recv()

    def result(self, i):
        own = self.blocks[self.me, i].astype(F32)
        return own + self.fin[0, i].astype(F32) + self.fin[1, i].astype(F32)

    def drain(self):
        for copy in self.first + self.second:
            copy.wait_send()


def share_kernel(
    table, offs, shares, matched, meta, out,
    core_out, core_in, relay1, fin1, blocks2, relay2, fin2, blocks3, far_in,
    meta_z, meta_x, meta_y, meta_c, send_sem, recv_sem,
):
    x, y, z, c = position()
    peers = [device_at(x, y, z, 1 - c)]
    peers += [device_at((x + d) % 4, y, z, c) for d in (1, 2, 3)]
    peers += [device_at(x, (y + d) % 4, z, c) for d in (1, 2, 3)]
    peers += [device_at(x, y, (z + d) % DEPTH, c) for d in range(1, DEPTH)]
    barrier = pltpu.get_barrier_semaphore()
    for peer in peers:
        pl.semaphore_signal(barrier, inc=1, device_id=peer, device_id_type=MESH)

    across_at = (iota((PIX, PPIX), 1) - iota((PIX, PPIX), 0)).astype(F32).astype(BF16)
    down_at = (iota((PPIX, PIX), 0) - iota((PPIX, PIX), 1)).astype(F32).astype(BF16)

    def one_hot(at, offset, share):
        full = lambda value: jnp.full(at.shape, value, F32).astype(BF16)
        offset = offset.astype(F32)
        second = jnp.where(at == full(offset + 1.0), full(share), full(0.0))
        return jnp.where(at == full(offset), full(1.0 - share), second)

    def place(q, r):
        slots = {}
        for i in range(4):
            for y_lo in range(2):
                z_to = lax.rem(z + distance_at(4 * q + i), DEPTH)
                p = z_to * 4 + y_lo * 2 + (c if r == 0 else 1 - c)
                for slot in range(2):
                    s = table[2 * p + slot]
                    filled = s >= 0
                    s = jnp.maximum(s, 0)
                    t, b = s % 2, s // 2
                    scale = jnp.where(filled, shares[4, b], 0.0)
                    across = one_hot(across_at, offs[t, 1, b], shares[2 * t + 1, b])
                    wide = jnp.dot(matched[b], across, preferred_element_type=F32)
                    slots[i, y_lo, slot] = (s, (scale * wide).astype(BF16))
        for i in range(4):
            for y_lo in range(2):
                downs = []
                for slot in range(2):
                    s = slots[i, y_lo, slot][0]
                    t, b = s % 2, s // 2
                    downs.append(one_hot(down_at, offs[t, 0, b], shares[2 * t, b]))
                tile = jnp.dot(
                    jnp.concatenate(downs, axis=1),
                    jnp.concatenate([slots[i, y_lo, slot][1] for slot in range(2)], axis=0),
                    preferred_element_type=F32,
                )
                for x_to in range(4):
                    for y_hi in range(2):
                        at = (x_to * 2 + y_hi) * ROWS
                        y_to = y_hi * 2 + y_lo
                        for half in range(2):
                            block = tile[at : at + ROWS, half * PIX : (half + 1) * PIX]
                            to = (x_to, i, y_to) if half == 0 else (y_to, i, x_to)
                            if r == 1:
                                core_out[(q, half) + to] = block.astype(BF16)
                            else:
                                block = block + core_in[(q, half) + to].astype(F32)
                                core_in[(q, half) + to] = block.astype(BF16)

    copies = Copies(send_sem, recv_sem)
    x_device = lambda to: device_at(to, y, z, c)
    y_device = lambda to: device_at(x, to, z, c)
    z_device = lambda k: device_at(x, y, (z + distance_at(k)) % DEPTH, c)

    core, meta_copies = [], []

    def send(q):
        place(q, 1)
        if q == 0:
            pl.semaphore_wait(barrier, len(peers))
        copy = copies.new(core_out.at[q], core_in.at[q], device_at(x, y, z, 1 - c))
        copy.start()
        core.append(copy)

    def meta_depth():
        for k in range(DEPTH - 1):
            copy = copies.new(meta.at[k], meta_z.at[k], z_device(k))
            copy.start()
            meta_copies.append(copy)
        meta_z[DEPTH - 1] = meta[DEPTH - 1]

    rings1, rings2, sent3 = {}, {}, []

    def enter(q):
        core[q].wait_recv()

        place(q, 0)
        for half in range(2):
            me, device = ((x, x_device), (y, y_device))[half]
            rings1[q, half] = Ring(
                copies, me, device, core_in.at[q, half], relay1.at[q, half], fin1.at[q, half]
            )
            rings1[q, half].start()

    def middle(q):
        for half in range(2):
            rings1[q, half].forward()

    def turn(q):
        for half in range(2):
            ring = rings1[q, half]
            ring.finish()
            for i in range(4):
                block = ring.result(i).astype(BF16)
                for other in range(4):
                    blocks2[q, half, other, i] = block[other]
            me, device = ((y, y_device), (x, x_device))[half]
            rings2[q, half] = Ring(
                copies, me, device, blocks2.at[q, half], relay2.at[q, half], fin2.at[q, half]
            )
            rings2[q, half].start()

    def middle2(q):
        for half in range(2):
            rings2[q, half].forward()

    def leave(q):
        for half in range(2):
            ring = rings2[q, half]
            ring.finish()
            for i in range(4):
                k = 4 * q + i
                if k < DEPTH - 1:
                    blocks3[k, half] = ring.result(i).astype(BF16)
                else:
                    far_in[k, half] = ring.result(i).astype(BF16)
        for i in range(4):
            k = 4 * q + i
            if k < DEPTH - 1:
                copy = copies.new(blocks3.at[k], far_in.at[k], z_device(k))
                copy.start()
                sent3.append(copy)

    def meta_plane():
        for copy in meta_copies:
            copy.wait_recv()
        total = meta_z[0]
        for k in range(1, DEPTH):
            total = total + meta_z[k]
        meta_x[x] = total
        sent = []
        for d in (1, 2, 3):
            sent.append(copies.new(meta_x.at[x], meta_x.at[x], x_device((x + d) % 4)))
        for copy in sent:
            copy.start()
        meta_copies.extend(sent)
        return sent

    def meta_second(before):
        for copy in before:
            copy.wait_recv()
        meta_y[y] = meta_x[...]
        sent = []
        for d in (1, 2, 3):
            sent.append(copies.new(meta_y.at[y], meta_y.at[y], y_device((y + d) % 4)))
        for copy in sent:
            copy.start()
        meta_copies.extend(sent)
        return sent

    def meta_third(before):
        for copy in before:
            copy.wait_recv()
        copy = copies.new(meta_y, meta_c, device_at(x, y, z, 1 - c))
        copy.start()
        meta_copies.append(copy)
        return copy

    send(0)
    send(1)
    meta_depth()
    enter(0)
    send(2)
    middle(0)
    enter(1)
    send(3)
    sent_x = meta_plane()
    turn(0)
    middle(1)
    enter(2)
    sent_y = meta_second(sent_x)
    middle2(0)
    turn(1)
    middle(2)
    enter(3)
    leave(0)
    sent_c = meta_third(sent_y)
    middle2(1)
    turn(2)
    middle(3)
    leave(1)
    middle2(2)
    turn(3)
    leave(2)
    middle2(3)

    sent_c.wait_recv()
    combo = (y % 2) * 2 + c
    lane = iota((8, PIX), 1)
    mine = (lane // 2) % 4 == combo
    row_at = (iota((ROWS, PIX), 0) + (x * 2 + y // 2) * ROWS).astype(F32)
    column_at = iota((PPIX, PIX), 0).astype(F32)

    def cover(at, offset, share):
        rest = (1.0 - share).astype(BF16).astype(F32)
        d = at - offset
        first = jnp.where((d >= 0.0) & (d < float(PIX)), rest, 0.0)
        return first + jnp.where((d >= 1.0) & (d < float(PIX + 1)), share, 0.0)

    weight = jnp.zeros((ROWS, PPIX), F32)
    for source in (meta_y, meta_c):
        for b in range(4):
            full = jnp.zeros((8, PIX), F32)
            for m in range(4):
                kept = jnp.where(mine, source[b, m], 0.0)
                full = full + pltpu.roll(kept, (2 * (m - combo)) % PIX, 1)
            valid = full[5:6] > 0.0
            inverse = jnp.where(valid, 1.0 / jnp.where(valid, full[4:5], 1.0), 0.0)
            down = inverse * cover(row_at, full[0:1], full[2:3])
            across = cover(column_at, full[1:2], full[3:4])
            weight = weight + lax.dot_general(
                down, across, (((1,), (1,)), ((), ())),
                precision=lax.Precision.HIGHEST, preferred_element_type=F32,
            )

    leave(3)
    for copy in sent3:
        copy.wait_recv()
    for half in range(2):
        total = far_in[0, half].astype(F32)
        for k in range(1, DEPTH):
            total = total + far_in[k, half].astype(F32)
        across = slice(half * PIX, (half + 1) * PIX)
        out[:, across] = total / jnp.sqrt(weight[:, across] + 1.0)

    for copy in core + meta_copies + sent3:
        copy.wait_send()
    for ring in list(rings1.values()) + list(rings2.values()):
        ring.drain()


COPY_COUNT = PARTS + PARTS * 24 + (DEPTH - 1) * 2 + 7


def body(images, intersection, offsets, subpixel, variance, basis_index, coefficients):
    inter = intersection[0].T
    offs = jnp.transpose(offsets[0], (1, 2, 0))
    frac = jnp.transpose(subpixel[0], (1, 2, 0))
    coef = jnp.transpose(coefficients, (1, 2, 0))
    smem = pl.BlockSpec(memory_space=pltpu.SMEM)
    vmem = pl.BlockSpec(memory_space=pltpu.VMEM)
    matched, table, shares, meta = pl.pallas_call(
        match_kernel,
        out_shape=(
            jax.ShapeDtypeStruct((CELLS, PIX, PIX), BF16),
            jax.ShapeDtypeStruct((2 * PATCHES,), I32),
            jax.ShapeDtypeStruct((8, PIX), F32),
            jax.ShapeDtypeStruct((DEPTH, 8, PIX), F32),
        ),
        in_specs=[smem] * 4 + [vmem] * 5,
        out_specs=(vmem, smem, smem, vmem),
        scratch_shapes=[
            pltpu.VMEM((8, PIX), F32),
            pltpu.SMEM((PATCHES,), I32),
            pltpu.SemaphoreType.DMA,
        ],
        compiler_params=pltpu.CompilerParams(vmem_limit_bytes=VMEM_LIMIT),
    )(inter, offs, basis_index, coef, images[0], inter, offs, frac, variance)
    out = pl.pallas_call(
        share_kernel,
        out_shape=jax.ShapeDtypeStruct((ROWS, PPIX), F32),
        in_specs=[smem] * 3 + [vmem] * 2,
        out_specs=vmem,
        scratch_shapes=[
            pltpu.VMEM((PARTS, 2, 4, 4, 4, ROWS, PIX), BF16),
            pltpu.VMEM((PARTS, 2, 4, 4, 4, ROWS, PIX), BF16),
            pltpu.VMEM((PARTS, 2, 2, 2, 4, ROWS, PIX), BF16),
            pltpu.VMEM((PARTS, 2, 2, 4, 4, ROWS, PIX), BF16),
            pltpu.VMEM((PARTS, 2, 4, 4, ROWS, PIX), BF16),
            pltpu.VMEM((PARTS, 2, 2, 2, ROWS, PIX), BF16),
            pltpu.VMEM((PARTS, 2, 2, 4, ROWS, PIX), BF16),
            pltpu.VMEM((DEPTH - 1, 2, ROWS, PIX), BF16),
            pltpu.VMEM((DEPTH, 2, ROWS, PIX), BF16),
            pltpu.VMEM((DEPTH, 8, PIX), F32),
            pltpu.VMEM((4, 8, PIX), F32),
            pltpu.VMEM((4, 4, 8, PIX), F32),
            pltpu.VMEM((4, 4, 8, PIX), F32),
            pltpu.SemaphoreType.DMA((COPY_COUNT,)),
            pltpu.SemaphoreType.DMA((COPY_COUNT,)),
        ],
        compiler_params=pltpu.CompilerParams(
            collective_id=0, has_side_effects=True, vmem_limit_bytes=VMEM_LIMIT
        ),
    )(table, offs, shares, matched, meta)
    return out[None]


def solution(mesh):
    return jax.shard_map(
        body,
        mesh=mesh,
        in_specs=(
            P("visit", "patch", None, None),
            P("visit", "patch", None),
            P("visit", "patch", None, None),
            P("visit", "patch", None, None),
            P("visit", "patch"),
            P("visit", "patch"),
            P(),
        ),
        out_specs=P("patch", "visit", None),
        check_vma=False,
    )
```

```python
import math

import jax
import jax.numpy as jnp
from jax import lax
from jax.experimental import pallas as pl
from jax.experimental.pallas import tpu as pltpu
from jax.sharding import PartitionSpec as P

PIX = 128
PPIX = 256
NB = 3
CELLS = 32
PATCHES = 64
DEPTH = 16
CHUNKS = (2, 4, 4, 4, 2)
ROWS = 32
F32, BF16, I32 = jnp.float32, jnp.bfloat16, jnp.int32
MESH = pl.DeviceIdType.MESH
GROUP = 8
VMEM_LIMIT = 56 * 1024 * 1024


def distance_at(k):
    if isinstance(k, int):
        return 8 + k // 2 if k % 2 == 0 else 7 - k // 2
    return jnp.where(k % 2 == 0, 8 + k // 2, 7 - k // 2)


def position():
    v, p = lax.axis_index("visit"), lax.axis_index("patch")
    return v // 2, (v % 2) * 2 + (p // 2) % 2, p // 4, p % 2


def device_at(x, y, z, c):
    return {"visit": x * 2 + y // 2, "patch": z * 4 + (y % 2) * 2 + c}


def iota(shape, axis):
    return lax.broadcasted_iota(I32, shape, axis)


class Copies:
    def __init__(self, send, recv):
        self.send, self.recv, self.used = send, recv, 0

    def new(self, src, dst, device):
        at = self.used
        self.used += 1
        return pltpu.make_async_remote_copy(
            src_ref=src,
            dst_ref=dst,
            send_sem=self.send.at[at],
            recv_sem=self.recv.at[at],
            device_id=device,
            device_id_type=MESH,
        )


def add_into(dst, src):
    dst[...] = (dst[...].astype(F32) + src[...].astype(F32)).astype(BF16)


class Ring:
    def __init__(self, copies, me, device, blocks, relay, fin):
        half = blocks.shape[1] // 2
        lo, hi = pl.ds(0, half), pl.ds(half, half)
        right, left, far = (me + 1) % 4, (me + 3) % 4, (me + 2) % 4
        to_right, to_left = device(right), device(left)
        self.blocks, self.relay, self.fin = blocks, relay, fin
        self.me, self.left, self.right, self.lo, self.hi = me, left, right, lo, hi
        self.first = [
            copies.new(blocks.at[far, lo], relay.at[0], to_right),
            copies.new(blocks.at[far, hi], relay.at[1], to_left),
            copies.new(blocks.at[right, hi], fin.at[0, hi], to_right),
            copies.new(blocks.at[left, lo], fin.at[1, lo], to_left),
        ]
        self.second = [
            copies.new(blocks.at[right, lo], fin.at[0, lo], to_right),
            copies.new(blocks.at[left, hi], fin.at[1, hi], to_left),
        ]

    def start(self):
        for copy in self.first:
            copy.start()

    def forward(self):
        self.first[0].wait_recv()
        add_into(self.blocks.at[self.right, self.lo], self.relay.at[0])
        self.second[0].start()
        self.first[1].wait_recv()
        add_into(self.blocks.at[self.left, self.hi], self.relay.at[1])
        self.second[1].start()

    def finish(self):
        for copy in self.first[2:] + self.second:
            copy.wait_recv()

    def result(self, i):
        own = self.blocks[self.me, i].astype(F32)
        return own + self.fin[0, i].astype(F32) + self.fin[1, i].astype(F32)

    def drain(self):
        for copy in self.first + self.second:
            copy.wait_send()


class Exchange:
    def __init__(self, copies, me, device, blocks, fin):
        self.me, self.blocks, self.fin = me, blocks, fin
        self.all = []
        for d in (2, 1, 3):
            to = (me + d) % 4
            self.all.append(copies.new(blocks.at[to], fin.at[d - 1], device(to)))

    def start(self):
        for copy in self.all:
            copy.start()

    def finish(self):
        for copy in self.all:
            copy.wait_recv()

    def result(self, i):
        total = self.blocks[self.me, i].astype(F32)
        for d in range(3):
            total = total + self.fin[d, i].astype(F32)
        return total

    def drain(self):
        for copy in self.all:
            copy.wait_send()


def coadd_kernel(
    basis, coef, images, inter, offs, frac, var, out,
    matched, slots_i, slots_f, table_i, table_f, meta, far_out, far_in,
    meta_z, meta_x, meta_y, meta_c, send_sem, recv_sem, move_sem, *chunk_refs,
):
    x, y, z, c = position()
    partner = device_at(x, y, z, 1 - c)
    x_device = lambda to: device_at(to, y, z, c)
    y_device = lambda to: device_at(x, to, z, c)
    z_device = lambda k: device_at(x, y, (z + distance_at(k)) % DEPTH, c)
    peers = [partner]
    peers += [x_device((x + d) % 4) for d in (1, 2, 3)]
    peers += [y_device((y + d) % 4) for d in (1, 2, 3)]
    peers += [z_device(k) for k in range(DEPTH - 1)]
    barrier = pltpu.get_barrier_semaphore()
    for peer in peers:
        pl.semaphore_signal(barrier, inc=1, device_id=peer, device_id_type=MESH)
    copies = Copies(send_sem, recv_sem)
    sent = []

    def start(copy):
        copy.start()
        sent.append(copy)
        return copy

    earlier = iota((CELLS, CELLS), 1) < iota((CELLS, CELLS), 0)
    diagonal = iota((CELLS, CELLS), 1) == iota((CELLS, CELLS), 0)
    lane = iota((CELLS, PIX), 1)
    cell = iota((CELLS, PIX), 0)
    row = iota((8, CELLS), 0)
    params = jnp.zeros((8, PIX), F32)
    cell_of = jnp.zeros((1, PIX), I32)
    for t in range(2):
        named = inter[t : t + 1]
        column = jnp.sum(jnp.where(diagonal, named, 0), axis=1, keepdims=True)
        code = 2 * column
        for other in range(2):
            same = (column == inter[other : other + 1]) & earlier
            code = code + jnp.sum(jnp.where(same, 1, 0), axis=1, keepdims=True)
        chosen = code == lane
        here = jnp.max(jnp.where(chosen, cell, 0), axis=0, keepdims=True)
        cell_of = jnp.maximum(cell_of, here)
        field = jnp.where(row == 0, offs[t, 0:1].astype(F32), 0.0)
        field = jnp.where(row == 1, offs[t, 1:2].astype(F32), field)
        field = jnp.where(row == 2, frac[t, 0:1].astype(F32), field)
        field = jnp.where(row == 3, frac[t, 1:2].astype(F32), field)
        field = jnp.where(row == 4, var[...].astype(F32), field)
        field = jnp.where(row == 5, 1.0, field).astype(BF16)
        pick = jnp.where(chosen, 1.0, 0.0).astype(BF16)
        params = params + jnp.dot(field, pick, preferred_element_type=F32)
    valid = params[5:6] > 0.0
    scale = jnp.where(valid, 1.0 / jnp.where(valid, params[4:5], 1.0), 0.0)
    slots_i[0] = jnp.broadcast_to(cell_of, (8, PIX))
    slots_f[0] = jnp.where(iota((8, PIX), 0) == 4, scale, params)
    own_moves = [
        pltpu.make_async_copy(slots_i.at[0], table_i.at[0], move_sem.at[0]),
        pltpu.make_async_copy(slots_f.at[0], table_f.at[0], move_sem.at[1]),
    ]
    for move in own_moves:
        move.start()
    my_lanes = iota((8, PIX), 1) // 8 == z
    for k in range(DEPTH):
        z_to = lax.rem(z + distance_at(k), DEPTH)
        turned = pltpu.roll(params, lax.rem(8 * (z - z_to) + PIX, PIX), 1)
        meta[k] = jnp.where(my_lanes, turned, 0.0)

    spread = (iota((PIX, PIX), 0) - iota((PIX, PIX), 1)).astype(F32)
    kernels = []
    for k in range(NB):
        width = 2.0**k
        profile = jnp.exp(-(spread**2) / (2.0 * width**2))
        kernels.append((profile / (math.sqrt(2.0 * math.pi) * width)).astype(BF16))
    stacked = jnp.concatenate(kernels, axis=1)
    ramp_i = (2.0 * iota((PIX, PIX), 0).astype(F32) - (PIX - 1)) / (PIX - 1)
    ramp_j = (2.0 * iota((PIX, PIX), 1).astype(F32) - (PIX - 1)) / (PIX - 1)

    def match(g):
        rows = jnp.dot(
            images[pl.ds(GROUP * g, GROUP)].reshape(GROUP * PIX, PIX),
            stacked,
            preferred_element_type=F32,
        ).astype(BF16)
        total = [None] * GROUP
        for k in range(NB):
            part = rows[:, k * PIX : (k + 1) * PIX]
            wide = jnp.concatenate([part[b * PIX : (b + 1) * PIX] for b in range(GROUP)], axis=1)
            smooth = jnp.dot(kernels[k], wide, preferred_element_type=F32)
            for b in range(GROUP):
                q = basis[0, GROUP * g + b]
                mix = coef[k, 0, q] + coef[k, 1, q] * ramp_i + coef[k, 2, q] * ramp_j
                term = mix * smooth[:, b * PIX : (b + 1) * PIX]
                total[b] = term if k == 0 else total[b] + term
        for b in range(GROUP):
            matched[0, GROUP * g + b] = total[b].astype(BF16)

    cells_in = []

    def send_cells(group):
        cells_in.append(start(copies.new(matched.at[0, group], matched.at[1, group], partner)))

    @pl.loop(0, 2)
    def _(g):
        match(g)

    pl.semaphore_wait(barrier, len(peers))
    send_cells(pl.ds(0, 2 * GROUP))
    tables_in = [
        start(copies.new(slots_i.at[0], slots_i.at[1], partner)),
        start(copies.new(slots_f.at[0], slots_f.at[1], partner)),
    ]
    depth_in = [start(copies.new(meta.at[k], meta_z.at[k], z_device(k))) for k in range(DEPTH - 1)]
    meta_z[DEPTH - 1] = meta[DEPTH - 1]
    for g in (2, 3):
        match(g)
        send_cells(pl.ds(g * GROUP, GROUP))

    for move in own_moves:
        move.wait()
    for copy in tables_in:
        copy.wait_recv()
    other_moves = [
        pltpu.make_async_copy(slots_i.at[1], table_i.at[1], move_sem.at[2]),
        pltpu.make_async_copy(slots_f.at[1], table_f.at[1], move_sem.at[3]),
    ]
    for move in other_moves:
        move.start()
    for move in other_moves:
        move.wait()
    for copy in cells_in:
        copy.wait_recv()

    across_at = (iota((PIX, PPIX), 1) - iota((PIX, PPIX), 0)).astype(F32).astype(BF16)
    down_at = (iota((PPIX, PIX), 0) - iota((PPIX, PIX), 1)).astype(F32).astype(BF16)

    def one_hot(at, offset, share):
        full = lambda value: jnp.full(at.shape, value, F32).astype(BF16)
        second = jnp.where(at == full(offset + 1.0), full(share), full(0.0))
        return jnp.where(at == full(offset), full(1.0 - share), second)

    count = len(CHUNKS)
    first = [sum(CHUNKS[:q]) for q in range(count)]
    refs = [chunk_refs[5 * q : 5 * q + 5] for q in range(count)]
    rings1, rings2, last = {}, {}, []

    def place(q, blocks):
        pieces = {}
        for i in range(CHUNKS[q]):
            z_to = lax.rem(z + distance_at(first[q] + i), DEPTH)
            for y_lo in range(2):
                slot = 2 * (z_to * 4 + y_lo * 2 + c)
                for source in range(2):
                    for r in range(2):
                        field = lambda f: table_f[source, f, slot + r]
                        across = one_hot(across_at, field(1), field(3))
                        wide = jnp.dot(
                            matched[source, table_i[source, 0, slot + r]],
                            across,
                            preferred_element_type=F32,
                        )
                        pieces[i, y_lo, source, r] = (field(4) * wide).astype(BF16)
        for i in range(CHUNKS[q]):
            z_to = lax.rem(z + distance_at(first[q] + i), DEPTH)
            for y_lo in range(2):
                slot = 2 * (z_to * 4 + y_lo * 2 + c)
                downs, placed = [], []
                for source in range(2):
                    for r in range(2):
                        field = lambda f: table_f[source, f, slot + r]
                        downs.append(one_hot(down_at, field(0), field(2)))
                        placed.append(pieces[i, y_lo, source, r])
                tile = jnp.dot(
                    jnp.concatenate(downs, axis=1),
                    jnp.concatenate(placed, axis=0),
                    preferred_element_type=F32,
                ).astype(BF16)
                for x_to in range(4):
                    for y_hi in range(2):
                        at = (x_to * 2 + y_hi) * ROWS
                        y_to = y_hi * 2 + y_lo
                        blocks[0, x_to, i, y_to] = tile[at : at + ROWS, :PIX]
                        blocks[1, y_to, i, x_to] = tile[at : at + ROWS, PIX:]

    def enter(q):
        blocks, relay, fin = refs[q][:3]
        place(q, blocks)
        for half in range(2):
            me, device = ((x, x_device), (y, y_device))[half]
            ring = Ring(copies, me, device, blocks.at[half], relay.at[half], fin.at[half])
            ring.start()
            rings1[q, half] = ring

    def forward(q):
        for half in range(2):
            rings1[q, half].forward()

    def turn(q):
        blocks, fin = refs[q][3:5]
        for half in range(2):
            ring = rings1[q, half]
            ring.finish()
            for i in range(CHUNKS[q]):
                block = ring.result(i).astype(BF16)
                for other in range(4):
                    blocks[half, other, i] = block[other]
            me, device = ((y, y_device), (x, x_device))[half]
            rings2[q, half] = Exchange(copies, me, device, blocks.at[half], fin.at[half])
            rings2[q, half].start()

    def leave(q):
        for half in range(2):
            ring = rings2[q, half]
            ring.finish()
            for i in range(CHUNKS[q]):
                k = first[q] + i
                to = far_out if k < DEPTH - 1 else far_in
                to[k, half] = ring.result(i).astype(BF16)
        for i in range(CHUNKS[q]):
            k = first[q] + i
            if k < DEPTH - 1:
                last.append(start(copies.new(far_out.at[k], far_in.at[k], z_device(k))))

    def meta_first():
        for copy in depth_in:
            copy.wait_recv()
        total = meta_z[0]
        for k in range(1, DEPTH):
            total = total + meta_z[k]
        meta_x[x] = total
        return [
            start(copies.new(meta_x.at[x], meta_x.at[x], x_device((x + d) % 4))) for d in (1, 2, 3)
        ]

    def meta_second(before):
        for copy in before:
            copy.wait_recv()
        meta_y[y] = meta_x[...]
        return [
            start(copies.new(meta_y.at[y], meta_y.at[y], y_device((y + d) % 4))) for d in (1, 2, 3)
        ]

    def meta_third(before):
        for copy in before:
            copy.wait_recv()
        return start(copies.new(meta_y, meta_c, partner))

    enter(0)
    enter(1)
    forward(0)
    enter(2)
    sent_x = meta_first()
    forward(1)
    turn(0)
    enter(3)
    sent_y = meta_second(sent_x)
    forward(2)
    turn(1)
    leave(0)
    enter(4)
    sent_c = meta_third(sent_y)
    forward(3)
    turn(2)
    leave(1)
    forward(4)
    turn(3)
    leave(2)

    sent_c.wait_recv()
    combo = (y % 2) * 2 + c
    mine = (iota((8, PIX), 1) // 2) % 4 == combo
    row_at = (iota((ROWS, PIX), 0) + (x * 2 + y // 2) * ROWS).astype(F32)
    column_at = iota((PPIX, PIX), 0).astype(F32)

    def cover(at, offset, share):
        rest = (1.0 - share).astype(BF16).astype(F32)
        d = at - offset
        once = jnp.where((d >= 0.0) & (d < float(PIX)), rest, 0.0)
        return once + jnp.where((d >= 1.0) & (d < float(PIX + 1)), share, 0.0)

    weight = jnp.zeros((ROWS, PPIX), F32)
    for source in (meta_y, meta_c):
        for b in range(4):
            full = jnp.zeros((8, PIX), F32)
            for m in range(4):
                kept = jnp.where(mine, source[b, m], 0.0)
                full = full + pltpu.roll(kept, lax.rem(2 * (m - combo) + PIX, PIX), 1)
            there = full[5:6] > 0.0
            inverse = jnp.where(there, 1.0 / jnp.where(there, full[4:5], 1.0), 0.0)
            down = inverse * cover(row_at, full[0:1], full[2:3])
            across = cover(column_at, full[1:2], full[3:4])
            weight = weight + lax.dot_general(
                down, across, (((1,), (1,)), ((), ())),
                precision=lax.Precision.HIGHEST, preferred_element_type=F32,
            )

    turn(4)
    leave(3)
    leave(4)
    for copy in last:
        copy.wait_recv()
    for half in range(2):
        total = far_in[0, half].astype(F32)
        for k in range(1, DEPTH):
            total = total + far_in[k, half].astype(F32)
        columns = slice(half * PIX, (half + 1) * PIX)
        out[:, columns] = total / jnp.sqrt(weight[:, columns] + 1.0)

    for copy in sent:
        copy.wait_send()
    for ring in list(rings1.values()) + list(rings2.values()):
        ring.drain()


COPY_COUNT = 3 + 2 + (DEPTH - 1) * 2 + 7 + len(CHUNKS) * 18


def chunk_shapes(n):
    return [
        pltpu.VMEM((2, 4, n, 4, ROWS, PIX), BF16),
        pltpu.VMEM((2, 2, n // 2, 4, ROWS, PIX), BF16),
        pltpu.VMEM((2, 2, n, 4, ROWS, PIX), BF16),
        pltpu.VMEM((2, 4, n, ROWS, PIX), BF16),
        pltpu.VMEM((2, 3, n, ROWS, PIX), BF16),
    ]


def body(images, intersection, offsets, subpixel, variance, basis_index, coefficients):
    smem = pl.BlockSpec(memory_space=pltpu.SMEM)
    vmem = pl.BlockSpec(memory_space=pltpu.VMEM)
    scratch = [
        pltpu.VMEM((2, CELLS, PIX, PIX), BF16),
        pltpu.VMEM((2, 8, PIX), I32),
        pltpu.VMEM((2, 8, PIX), F32),
        pltpu.SMEM((2, 8, PIX), I32),
        pltpu.SMEM((2, 8, PIX), F32),
        pltpu.VMEM((DEPTH, 8, PIX), F32),
        pltpu.VMEM((DEPTH - 1, 2, ROWS, PIX), BF16),
        pltpu.VMEM((DEPTH, 2, ROWS, PIX), BF16),
        pltpu.VMEM((DEPTH, 8, PIX), F32),
        pltpu.VMEM((4, 8, PIX), F32),
        pltpu.VMEM((4, 4, 8, PIX), F32),
        pltpu.VMEM((4, 4, 8, PIX), F32),
        pltpu.SemaphoreType.DMA((COPY_COUNT,)),
        pltpu.SemaphoreType.DMA((COPY_COUNT,)),
        pltpu.SemaphoreType.DMA((4,)),
    ]
    for n in CHUNKS:
        scratch += chunk_shapes(n)
    out = pl.pallas_call(
        coadd_kernel,
        out_shape=jax.ShapeDtypeStruct((ROWS, PPIX), F32),
        in_specs=[smem] * 2 + [vmem] * 5,
        out_specs=vmem,
        scratch_shapes=scratch,
        compiler_params=pltpu.CompilerParams(
            collective_id=0, has_side_effects=True, vmem_limit_bytes=VMEM_LIMIT
        ),
    )(
        basis_index,
        jnp.transpose(coefficients, (1, 2, 0)),
        images[0],
        intersection[0].T,
        jnp.transpose(offsets[0], (1, 2, 0)),
        jnp.transpose(subpixel[0], (1, 2, 0)),
        variance,
    )
    return out[None]


def solution(mesh):
    return jax.shard_map(
        body,
        mesh=mesh,
        in_specs=(
            P("visit", "patch", None, None),
            P("visit", "patch", None),
            P("visit", "patch", None, None),
            P("visit", "patch", None, None),
            P("visit", "patch"),
            P("visit", "patch"),
            P(),
        ),
        out_specs=P("patch", "visit", None),
        check_vma=False,
    )
```

```python
import math

import jax
import jax.numpy as jnp
from jax import lax
from jax.experimental import pallas as pl
from jax.experimental.pallas import tpu as pltpu
from jax.sharding import PartitionSpec as P

PIX = 128
PPIX = 256
NB = 3
CELLS = 32
PATCHES = 64
DEPTH = 16
CHUNKS = (2, 4, 4, 4, 2)
ROWS = 32
F32, BF16, I32 = jnp.float32, jnp.bfloat16, jnp.int32
MESH = pl.DeviceIdType.MESH
GROUP = 8
VMEM_LIMIT = 56 * 1024 * 1024


def distance_at(k):
    if isinstance(k, int):
        return 8 + k // 2 if k % 2 == 0 else 7 - k // 2
    return jnp.where(k % 2 == 0, 8 + k // 2, 7 - k // 2)


def position():
    v, p = lax.axis_index("visit"), lax.axis_index("patch")
    return v // 2, (v % 2) * 2 + (p // 2) % 2, p // 4, p % 2


def device_at(x, y, z, c):
    return {"visit": x * 2 + y // 2, "patch": z * 4 + (y % 2) * 2 + c}


def iota(shape, axis):
    return lax.broadcasted_iota(I32, shape, axis)


class Copies:
    def __init__(self, send, recv):
        self.send, self.recv, self.used = send, recv, 0

    def new(self, src, dst, device):
        at = self.used
        self.used += 1
        return pltpu.make_async_remote_copy(
            src_ref=src,
            dst_ref=dst,
            send_sem=self.send.at[at],
            recv_sem=self.recv.at[at],
            device_id=device,
            device_id_type=MESH,
        )


def add_into(dst, src):
    dst[...] = (dst[...].astype(F32) + src[...].astype(F32)).astype(BF16)


class Ring:
    def __init__(self, copies, me, device, blocks, relay, fin):
        half = blocks.shape[1] // 2
        lo, hi = pl.ds(0, half), pl.ds(half, half)
        right, left, far = (me + 1) % 4, (me + 3) % 4, (me + 2) % 4
        to_right, to_left = device(right), device(left)
        self.blocks, self.relay, self.fin = blocks, relay, fin
        self.me, self.left, self.right, self.lo, self.hi = me, left, right, lo, hi
        self.first = [
            copies.new(blocks.at[far, lo], relay.at[0], to_right),
            copies.new(blocks.at[far, hi], relay.at[1], to_left),
            copies.new(blocks.at[right, hi], fin.at[0, hi], to_right),
            copies.new(blocks.at[left, lo], fin.at[1, lo], to_left),
        ]
        self.second = [
            copies.new(blocks.at[right, lo], fin.at[0, lo], to_right),
            copies.new(blocks.at[left, hi], fin.at[1, hi], to_left),
        ]

    def start(self):
        for copy in self.first:
            copy.start()

    def forward(self):
        self.first[0].wait_recv()
        add_into(self.blocks.at[self.right, self.lo], self.relay.at[0])
        self.second[0].start()
        self.first[1].wait_recv()
        add_into(self.blocks.at[self.left, self.hi], self.relay.at[1])
        self.second[1].start()

    def finish(self):
        for copy in self.first[2:] + self.second:
            copy.wait_recv()

    def result(self, i):
        own = self.blocks[self.me, i].astype(F32)
        return own + self.fin[0, i].astype(F32) + self.fin[1, i].astype(F32)

    def drain(self):
        for copy in self.first + self.second:
            copy.wait_send()


class Exchange:
    def __init__(self, copies, me, device, blocks, fin):
        self.me, self.blocks, self.fin = me, blocks, fin
        self.all = []
        for d in (2, 1, 3):
            to = (me + d) % 4
            self.all.append(copies.new(blocks.at[to], fin.at[d - 1], device(to)))

    def start(self):
        for copy in self.all:
            copy.start()

    def finish(self):
        for copy in self.all:
            copy.wait_recv()

    def result(self, i):
        total = self.blocks[self.me, i].astype(F32)
        for d in range(3):
            total = total + self.fin[d, i].astype(F32)
        return total

    def drain(self):
        for copy in self.all:
            copy.wait_send()


def coadd_kernel(
    basis, coef, images, inter, offs, frac, var, out,
    pixels, matched, slots_i, slots_f, table_i, table_f, meta, far_out, far_in,
    meta_z, meta_x, meta_y, meta_c, send_sem, recv_sem, move_sem, *chunk_refs,
):
    x, y, z, c = position()
    partner = device_at(x, y, z, 1 - c)
    x_device = lambda to: device_at(to, y, z, c)
    y_device = lambda to: device_at(x, to, z, c)
    z_device = lambda k: device_at(x, y, (z + distance_at(k)) % DEPTH, c)
    peers = [z_device(k) for k in range(DEPTH - 1)]
    peers += [x_device((x + d) % 4) for d in (2, 1, 3)]
    peers += [y_device((y + d) % 4) for d in (2, 1, 3)]
    peers += [partner]
    barrier = pltpu.get_barrier_semaphore()
    for peer in peers:
        pl.semaphore_signal(barrier, inc=1, device_id=peer, device_id_type=MESH)
    copies = Copies(send_sem, recv_sem)
    sent = []

    def pixels_in(g):
        cells = pl.ds(g * GROUP, GROUP)
        return pltpu.make_async_copy(images.at[cells], pixels.at[cells], move_sem.at[4 + g])

    for g in range(CELLS // GROUP):
        pixels_in(g).start()

    def start(copy):
        copy.start()
        sent.append(copy)
        return copy

    earlier = iota((CELLS, CELLS), 1) < iota((CELLS, CELLS), 0)
    diagonal = iota((CELLS, CELLS), 1) == iota((CELLS, CELLS), 0)
    lane = iota((CELLS, PIX), 1)
    cell = iota((CELLS, PIX), 0)
    row = iota((8, CELLS), 0)
    params = jnp.zeros((8, PIX), F32)
    cell_of = jnp.zeros((1, PIX), I32)
    for t in range(2):
        named = inter[t : t + 1]
        column = jnp.sum(jnp.where(diagonal, named, 0), axis=1, keepdims=True)
        code = 2 * column
        for other in range(2):
            same = (column == inter[other : other + 1]) & earlier
            code = code + jnp.sum(jnp.where(same, 1, 0), axis=1, keepdims=True)
        chosen = code == lane
        here = jnp.max(jnp.where(chosen, cell, 0), axis=0, keepdims=True)
        cell_of = jnp.maximum(cell_of, here)
        field = jnp.where(row == 0, offs[t, 0:1].astype(F32), 0.0)
        field = jnp.where(row == 1, offs[t, 1:2].astype(F32), field)
        field = jnp.where(row == 2, frac[t, 0:1].astype(F32), field)
        field = jnp.where(row == 3, frac[t, 1:2].astype(F32), field)
        field = jnp.where(row == 4, var[...].astype(F32), field)
        field = jnp.where(row == 5, 1.0, field).astype(BF16)
        pick = jnp.where(chosen, 1.0, 0.0).astype(BF16)
        params = params + jnp.dot(field, pick, preferred_element_type=F32)
    valid = params[5:6] > 0.0
    scale = jnp.where(valid, 1.0 / jnp.where(valid, params[4:5], 1.0), 0.0)
    slots_i[0] = jnp.broadcast_to(cell_of, (8, PIX))
    slots_f[0] = jnp.where(iota((8, PIX), 0) == 4, scale, params)
    own_moves = [
        pltpu.make_async_copy(slots_i.at[0], table_i.at[0], move_sem.at[0]),
        pltpu.make_async_copy(slots_f.at[0], table_f.at[0], move_sem.at[1]),
    ]
    for move in own_moves:
        move.start()
    my_lanes = iota((8, PIX), 1) // 8 == z
    for k in range(DEPTH):
        z_to = lax.rem(z + distance_at(k), DEPTH)
        turned = pltpu.roll(params, lax.rem(8 * (z - z_to) + PIX, PIX), 1)
        meta[k] = jnp.where(my_lanes, turned, 0.0)

    spread = (iota((PIX, PIX), 0) - iota((PIX, PIX), 1)).astype(F32)
    kernels = []
    for k in range(NB):
        width = 2.0**k
        profile = jnp.exp(-(spread**2) / (2.0 * width**2))
        kernels.append((profile / (math.sqrt(2.0 * math.pi) * width)).astype(BF16))
    stacked = jnp.concatenate(kernels, axis=1)
    ramp_i = (2.0 * iota((PIX, PIX), 0).astype(F32) - (PIX - 1)) / (PIX - 1)
    ramp_j = (2.0 * iota((PIX, PIX), 1).astype(F32) - (PIX - 1)) / (PIX - 1)

    def match(g):
        pixels_in(g).wait()
        rows = jnp.dot(
            pixels[pl.ds(GROUP * g, GROUP)].reshape(GROUP * PIX, PIX),
            stacked,
            preferred_element_type=F32,
        ).astype(BF16)
        total = [None] * GROUP
        for k in range(NB):
            part = rows[:, k * PIX : (k + 1) * PIX]
            wide = jnp.concatenate([part[b * PIX : (b + 1) * PIX] for b in range(GROUP)], axis=1)
            smooth = jnp.dot(kernels[k], wide, preferred_element_type=F32)
            for b in range(GROUP):
                q = basis[0, GROUP * g + b]
                mix = coef[k, 0, q] + coef[k, 1, q] * ramp_i + coef[k, 2, q] * ramp_j
                term = mix * smooth[:, b * PIX : (b + 1) * PIX]
                total[b] = term if k == 0 else total[b] + term
        for b in range(GROUP):
            matched[0, GROUP * g + b] = total[b].astype(BF16)

    cells_in = []

    def send_cells(group):
        cells_in.append(start(copies.new(matched.at[0, group], matched.at[1, group], partner)))

    @pl.loop(0, 2)
    def _(g):
        match(g)

    pl.semaphore_wait(barrier, len(peers))
    send_cells(pl.ds(0, 2 * GROUP))
    tables_in = [
        start(copies.new(slots_i.at[0], slots_i.at[1], partner)),
        start(copies.new(slots_f.at[0], slots_f.at[1], partner)),
    ]
    depth_in = [start(copies.new(meta.at[k], meta_z.at[k], z_device(k))) for k in range(DEPTH - 1)]
    meta_z[DEPTH - 1] = meta[DEPTH - 1]
    for g in (2, 3):
        match(g)
        send_cells(pl.ds(g * GROUP, GROUP))

    for move in own_moves:
        move.wait()
    for copy in tables_in:
        copy.wait_recv()
    other_moves = [
        pltpu.make_async_copy(slots_i.at[1], table_i.at[1], move_sem.at[2]),
        pltpu.make_async_copy(slots_f.at[1], table_f.at[1], move_sem.at[3]),
    ]
    for move in other_moves:
        move.start()
    for move in other_moves:
        move.wait()
    for copy in cells_in:
        copy.wait_recv()

    across_at = (iota((PIX, PPIX), 1) - iota((PIX, PPIX), 0)).astype(F32).astype(BF16)
    down_at = (iota((PPIX, PIX), 0) - iota((PPIX, PIX), 1)).astype(F32).astype(BF16)

    def one_hot(at, offset, share):
        full = lambda value: jnp.full(at.shape, value, F32).astype(BF16)
        second = jnp.where(at == full(offset + 1.0), full(share), full(0.0))
        return jnp.where(at == full(offset), full(1.0 - share), second)

    count = len(CHUNKS)
    first = [sum(CHUNKS[:q]) for q in range(count)]
    refs = [chunk_refs[5 * q : 5 * q + 5] for q in range(count)]
    rings1, rings2, last = {}, {}, []

    def place(q, blocks):
        pieces = {}
        for i in range(CHUNKS[q]):
            z_to = lax.rem(z + distance_at(first[q] + i), DEPTH)
            for y_lo in range(2):
                slot = 2 * (z_to * 4 + y_lo * 2 + c)
                for source in range(2):
                    for r in range(2):
                        field = lambda f: table_f[source, f, slot + r]
                        across = one_hot(across_at, field(1), field(3))
                        wide = jnp.dot(
                            matched[source, table_i[source, 0, slot + r]],
                            across,
                            preferred_element_type=F32,
                        )
                        pieces[i, y_lo, source, r] = (field(4) * wide).astype(BF16)
        for i in range(CHUNKS[q]):
            z_to = lax.rem(z + distance_at(first[q] + i), DEPTH)
            for y_lo in range(2):
                slot = 2 * (z_to * 4 + y_lo * 2 + c)
                downs, placed = [], []
                for source in range(2):
                    for r in range(2):
                        field = lambda f: table_f[source, f, slot + r]
                        downs.append(one_hot(down_at, field(0), field(2)))
                        placed.append(pieces[i, y_lo, source, r])
                tile = jnp.dot(
                    jnp.concatenate(downs, axis=1),
                    jnp.concatenate(placed, axis=0),
                    preferred_element_type=F32,
                ).astype(BF16)
                for x_to in range(4):
                    for y_hi in range(2):
                        at = (x_to * 2 + y_hi) * ROWS
                        y_to = y_hi * 2 + y_lo
                        blocks[0, x_to, i, y_to] = tile[at : at + ROWS, :PIX]
                        blocks[1, y_to, i, x_to] = tile[at : at + ROWS, PIX:]

    def enter(q):
        blocks, relay, fin = refs[q][:3]
        place(q, blocks)
        for half in range(2):
            me, device = ((x, x_device), (y, y_device))[half]
            ring = Ring(copies, me, device, blocks.at[half], relay.at[half], fin.at[half])
            ring.start()
            rings1[q, half] = ring

    def forward(q):
        for half in range(2):
            rings1[q, half].forward()

    def turn(q):
        blocks, fin = refs[q][3:5]
        for half in range(2):
            ring = rings1[q, half]
            ring.finish()
            for i in range(CHUNKS[q]):
                block = ring.result(i).astype(BF16)
                for other in range(4):
                    blocks[half, other, i] = block[other]
            me, device = ((y, y_device), (x, x_device))[half]
            rings2[q, half] = Exchange(copies, me, device, blocks.at[half], fin.at[half])
            rings2[q, half].start()

    def leave(q):
        for half in range(2):
            ring = rings2[q, half]
            ring.finish()
            for i in range(CHUNKS[q]):
                k = first[q] + i
                to = far_out if k < DEPTH - 1 else far_in
                to[k, half] = ring.result(i).astype(BF16)
        for i in range(CHUNKS[q]):
            k = first[q] + i
            if k < DEPTH - 1:
                last.append(start(copies.new(far_out.at[k], far_in.at[k], z_device(k))))

    def meta_first():
        for copy in depth_in:
            copy.wait_recv()
        total = meta_z[0]
        for k in range(1, DEPTH):
            total = total + meta_z[k]
        meta_x[x] = total
        return [
            start(copies.new(meta_x.at[x], meta_x.at[x], x_device((x + d) % 4))) for d in (1, 2, 3)
        ]

    def meta_second(before):
        for copy in before:
            copy.wait_recv()
        meta_y[y] = meta_x[...]
        return [
            start(copies.new(meta_y.at[y], meta_y.at[y], y_device((y + d) % 4))) for d in (1, 2, 3)
        ]

    def meta_third(before):
        for copy in before:
            copy.wait_recv()
        return start(copies.new(meta_y, meta_c, partner))

    enter(0)
    enter(1)
    forward(0)
    enter(2)
    sent_x = meta_first()
    forward(1)
    turn(0)
    enter(3)
    sent_y = meta_second(sent_x)
    forward(2)
    turn(1)
    leave(0)
    enter(4)
    sent_c = meta_third(sent_y)
    forward(3)
    turn(2)
    leave(1)
    forward(4)
    turn(3)
    leave(2)

    sent_c.wait_recv()
    combo = (y % 2) * 2 + c
    mine = (iota((8, PIX), 1) // 2) % 4 == combo
    row_at = (iota((ROWS, PIX), 0) + (x * 2 + y // 2) * ROWS).astype(F32)
    column_at = iota((PPIX, PIX), 0).astype(F32)

    def cover(at, offset, share):
        rest = (1.0 - share).astype(BF16).astype(F32)
        d = at - offset
        once = jnp.where((d >= 0.0) & (d < float(PIX)), rest, 0.0)
        return once + jnp.where((d >= 1.0) & (d < float(PIX + 1)), share, 0.0)

    weight = jnp.zeros((ROWS, PPIX), F32)
    for source in (meta_y, meta_c):
        for b in range(4):
            full = jnp.zeros((8, PIX), F32)
            for m in range(4):
                kept = jnp.where(mine, source[b, m], 0.0)
                full = full + pltpu.roll(kept, lax.rem(2 * (m - combo) + PIX, PIX), 1)
            there = full[5:6] > 0.0
            inverse = jnp.where(there, 1.0 / jnp.where(there, full[4:5], 1.0), 0.0)
            down = inverse * cover(row_at, full[0:1], full[2:3])
            across = cover(column_at, full[1:2], full[3:4])
            weight = weight + lax.dot_general(
                down, across, (((1,), (1,)), ((), ())),
                precision=lax.Precision.HIGHEST, preferred_element_type=F32,
            )

    turn(4)
    leave(3)
    leave(4)
    for copy in last:
        copy.wait_recv()
    for half in range(2):
        total = far_in[0, half].astype(F32)
        for k in range(1, DEPTH):
            total = total + far_in[k, half].astype(F32)
        columns = slice(half * PIX, (half + 1) * PIX)
        out[:, columns] = total / jnp.sqrt(weight[:, columns] + 1.0)

    for copy in sent:
        copy.wait_send()
    for ring in list(rings1.values()) + list(rings2.values()):
        ring.drain()


COPY_COUNT = 3 + 2 + (DEPTH - 1) * 2 + 7 + len(CHUNKS) * 18


def chunk_shapes(n):
    return [
        pltpu.VMEM((2, 4, n, 4, ROWS, PIX), BF16),
        pltpu.VMEM((2, 2, n // 2, 4, ROWS, PIX), BF16),
        pltpu.VMEM((2, 2, n, 4, ROWS, PIX), BF16),
        pltpu.VMEM((2, 4, n, ROWS, PIX), BF16),
        pltpu.VMEM((2, 3, n, ROWS, PIX), BF16),
    ]


def body(images, intersection, offsets, subpixel, variance, basis_index, coefficients):
    smem = pl.BlockSpec(memory_space=pltpu.SMEM)
    vmem = pl.BlockSpec(memory_space=pltpu.VMEM)
    scratch = [
        pltpu.VMEM((CELLS, PIX, PIX), BF16),
        pltpu.VMEM((2, CELLS, PIX, PIX), BF16),
        pltpu.VMEM((2, 8, PIX), I32),
        pltpu.VMEM((2, 8, PIX), F32),
        pltpu.SMEM((2, 8, PIX), I32),
        pltpu.SMEM((2, 8, PIX), F32),
        pltpu.VMEM((DEPTH, 8, PIX), F32),
        pltpu.VMEM((DEPTH - 1, 2, ROWS, PIX), BF16),
        pltpu.VMEM((DEPTH, 2, ROWS, PIX), BF16),
        pltpu.VMEM((DEPTH, 8, PIX), F32),
        pltpu.VMEM((4, 8, PIX), F32),
        pltpu.VMEM((4, 4, 8, PIX), F32),
        pltpu.VMEM((4, 4, 8, PIX), F32),
        pltpu.SemaphoreType.DMA((COPY_COUNT,)),
        pltpu.SemaphoreType.DMA((COPY_COUNT,)),
        pltpu.SemaphoreType.DMA((4 + CELLS // GROUP,)),
    ]
    for n in CHUNKS:
        scratch += chunk_shapes(n)
    out = pl.pallas_call(
        coadd_kernel,
        out_shape=jax.ShapeDtypeStruct((ROWS, PPIX), F32),
        in_specs=[smem] * 2 + [pl.BlockSpec(memory_space=pl.ANY)] + [vmem] * 4,
        out_specs=vmem,
        scratch_shapes=scratch,
        compiler_params=pltpu.CompilerParams(
            collective_id=0, has_side_effects=True, vmem_limit_bytes=VMEM_LIMIT
        ),
    )(
        basis_index,
        jnp.transpose(coefficients, (1, 2, 0)),
        images[0],
        intersection[0].T,
        jnp.transpose(offsets[0], (1, 2, 0)),
        jnp.transpose(subpixel[0], (1, 2, 0)),
        variance,
    )
    return out[None]


def solution(mesh):
    return jax.shard_map(
        body,
        mesh=mesh,
        in_specs=(
            P("visit", "patch", None, None),
            P("visit", "patch", None),
            P("visit", "patch", None, None),
            P("visit", "patch", None, None),
            P("visit", "patch"),
            P("visit", "patch"),
            P(),
        ),
        out_specs=P("patch", "visit", None),
        check_vma=False,
    )
```

```python
import math

import jax
import jax.numpy as jnp
from jax import lax
from jax.experimental import pallas as pl
from jax.experimental.pallas import tpu as pltpu
from jax.sharding import PartitionSpec as P

PIX = 128
PPIX = 256
NB = 3
CELLS = 32
PATCHES = 64
DEPTH = 16
CHUNKS = (2, 4, 4, 4, 2)
RING_PARTS = 3
ROWS = 32
F32, BF16, I32 = jnp.float32, jnp.bfloat16, jnp.int32
MESH = pl.DeviceIdType.MESH
GROUP = 8
VMEM_LIMIT = 56 * 1024 * 1024


def distance_at(k):
    if isinstance(k, int):
        return 8 + k // 2 if k % 2 == 0 else 7 - k // 2
    return jnp.where(k % 2 == 0, 8 + k // 2, 7 - k // 2)


def position():
    v, p = lax.axis_index("visit"), lax.axis_index("patch")
    return v // 2, (v % 2) * 2 + (p // 2) % 2, p // 4, p % 2


def device_at(x, y, z, c):
    return {"visit": x * 2 + y // 2, "patch": z * 4 + (y % 2) * 2 + c}


def iota(shape, axis):
    return lax.broadcasted_iota(I32, shape, axis)


class Copies:
    def __init__(self, send, recv):
        self.send, self.recv, self.used = send, recv, 0

    def new(self, src, dst, device):
        at = self.used
        self.used += 1
        return pltpu.make_async_remote_copy(
            src_ref=src,
            dst_ref=dst,
            send_sem=self.send.at[at],
            recv_sem=self.recv.at[at],
            device_id=device,
            device_id_type=MESH,
        )


def add_into(dst, src):
    dst[...] = (dst[...].astype(F32) + src[...].astype(F32)).astype(BF16)


class Ring:
    def __init__(self, copies, me, device, blocks, relay, fin):
        half = blocks.shape[1] // 2
        lo, hi = pl.ds(0, half), pl.ds(half, half)
        right, left, far = (me + 1) % 4, (me + 3) % 4, (me + 2) % 4
        to_right, to_left = device(right), device(left)
        self.blocks, self.relay, self.fin = blocks, relay, fin
        self.me, self.left, self.right, self.lo, self.hi = me, left, right, lo, hi
        self.first = [
            copies.new(blocks.at[far, lo], relay.at[0], to_right),
            copies.new(blocks.at[far, hi], relay.at[1], to_left),
            copies.new(blocks.at[right, hi], fin.at[0, hi], to_right),
            copies.new(blocks.at[left, lo], fin.at[1, lo], to_left),
        ]
        self.second = [
            copies.new(blocks.at[right, lo], fin.at[0, lo], to_right),
            copies.new(blocks.at[left, hi], fin.at[1, hi], to_left),
        ]

    def start(self):
        for copy in self.first:
            copy.start()

    def forward(self):
        self.first[0].wait_recv()
        add_into(self.blocks.at[self.right, self.lo], self.relay.at[0])
        self.second[0].start()
        self.first[1].wait_recv()
        add_into(self.blocks.at[self.left, self.hi], self.relay.at[1])
        self.second[1].start()

    def finish(self):
        for copy in self.first[2:] + self.second:
            copy.wait_recv()

    def result(self, i):
        own = self.blocks[self.me, i].astype(F32)
        return own + self.fin[0, i].astype(F32) + self.fin[1, i].astype(F32)

    def drain(self):
        for copy in self.first + self.second:
            copy.wait_send()


class Exchange:
    def __init__(self, copies, me, device, blocks, fin):
        self.me, self.blocks, self.fin = me, blocks, fin
        self.all = []
        for d in (2, 1, 3):
            to = (me + d) % 4
            self.all.append(copies.new(blocks.at[to], fin.at[d - 1], device(to)))

    def start(self):
        for copy in self.all:
            copy.start()

    def finish(self):
        for copy in self.all:
            copy.wait_recv()

    def result(self, i):
        total = self.blocks[self.me, i].astype(F32)
        for d in range(3):
            total = total + self.fin[d, i].astype(F32)
        return total

    def drain(self):
        for copy in self.all:
            copy.wait_send()


def coadd_kernel(
    basis, coef, images, inter, offs, frac, var, out,
    matched, slots_i, slots_f, table_i, table_f, meta, far_out, far_in,
    meta_z, meta_x, meta_y, meta_c, send_sem, recv_sem, move_sem, *chunk_refs,
):
    x, y, z, c = position()
    partner = device_at(x, y, z, 1 - c)
    x_device = lambda to: device_at(to, y, z, c)
    y_device = lambda to: device_at(x, to, z, c)
    z_device = lambda k: device_at(x, y, (z + distance_at(k)) % DEPTH, c)
    peers = [partner]
    peers += [x_device((x + d) % 4) for d in (1, 2, 3)]
    peers += [y_device((y + d) % 4) for d in (1, 2, 3)]
    peers += [z_device(k) for k in range(DEPTH - 1)]
    barrier = pltpu.get_barrier_semaphore()
    for peer in peers:
        pl.semaphore_signal(barrier, inc=1, device_id=peer, device_id_type=MESH)
    copies = Copies(send_sem, recv_sem)
    sent = []

    def start(copy):
        copy.start()
        sent.append(copy)
        return copy

    earlier = iota((CELLS, CELLS), 1) < iota((CELLS, CELLS), 0)
    diagonal = iota((CELLS, CELLS), 1) == iota((CELLS, CELLS), 0)
    lane = iota((CELLS, PIX), 1)
    cell = iota((CELLS, PIX), 0)
    row = iota((8, CELLS), 0)
    params = jnp.zeros((8, PIX), F32)
    cell_of = jnp.zeros((1, PIX), I32)
    for t in range(2):
        named = inter[t : t + 1]
        column = jnp.sum(jnp.where(diagonal, named, 0), axis=1, keepdims=True)
        code = 2 * column
        for other in range(2):
            same = (column == inter[other : other + 1]) & earlier
            code = code + jnp.sum(jnp.where(same, 1, 0), axis=1, keepdims=True)
        chosen = code == lane
        here = jnp.max(jnp.where(chosen, cell, 0), axis=0, keepdims=True)
        cell_of = jnp.maximum(cell_of, here)
        field = jnp.where(row == 0, offs[t, 0:1].astype(F32), 0.0)
        field = jnp.where(row == 1, offs[t, 1:2].astype(F32), field)
        field = jnp.where(row == 2, frac[t, 0:1].astype(F32), field)
        field = jnp.where(row == 3, frac[t, 1:2].astype(F32), field)
        field = jnp.where(row == 4, var[...].astype(F32), field)
        field = jnp.where(row == 5, 1.0, field).astype(BF16)
        pick = jnp.where(chosen, 1.0, 0.0).astype(BF16)
        params = params + jnp.dot(field, pick, preferred_element_type=F32)
    valid = params[5:6] > 0.0
    scale = jnp.where(valid, 1.0 / jnp.where(valid, params[4:5], 1.0), 0.0)
    slots_i[0] = jnp.broadcast_to(cell_of, (8, PIX))
    slots_f[0] = jnp.where(iota((8, PIX), 0) == 4, scale, params)
    own_moves = [
        pltpu.make_async_copy(slots_i.at[0], table_i.at[0], move_sem.at[0]),
        pltpu.make_async_copy(slots_f.at[0], table_f.at[0], move_sem.at[1]),
    ]
    for move in own_moves:
        move.start()
    my_lanes = iota((8, PIX), 1) // 8 == z
    for k in range(DEPTH):
        z_to = lax.rem(z + distance_at(k), DEPTH)
        turned = pltpu.roll(params, lax.rem(8 * (z - z_to) + PIX, PIX), 1)
        meta[k] = jnp.where(my_lanes, turned, 0.0)

    spread = (iota((PIX, PIX), 0) - iota((PIX, PIX), 1)).astype(F32)
    kernels = []
    for k in range(NB):
        width = 2.0**k
        profile = jnp.exp(-(spread**2) / (2.0 * width**2))
        kernels.append((profile / (math.sqrt(2.0 * math.pi) * width)).astype(BF16))
    stacked = jnp.concatenate(kernels, axis=1)
    ramp_i = (2.0 * iota((PIX, PIX), 0).astype(F32) - (PIX - 1)) / (PIX - 1)
    ramp_j = (2.0 * iota((PIX, PIX), 1).astype(F32) - (PIX - 1)) / (PIX - 1)

    def match(g):
        rows = jnp.dot(
            images[pl.ds(GROUP * g, GROUP)].reshape(GROUP * PIX, PIX),
            stacked,
            preferred_element_type=F32,
        ).astype(BF16)
        total = [None] * GROUP
        for k in range(NB):
            part = rows[:, k * PIX : (k + 1) * PIX]
            wide = jnp.concatenate([part[b * PIX : (b + 1) * PIX] for b in range(GROUP)], axis=1)
            smooth = jnp.dot(kernels[k], wide, preferred_element_type=F32)
            for b in range(GROUP):
                q = basis[0, GROUP * g + b]
                mix = coef[k, 0, q] + coef[k, 1, q] * ramp_i + coef[k, 2, q] * ramp_j
                term = mix * smooth[:, b * PIX : (b + 1) * PIX]
                total[b] = term if k == 0 else total[b] + term
        for b in range(GROUP):
            matched[0, GROUP * g + b] = total[b].astype(BF16)

    cells_in = []

    def send_cells(group):
        cells_in.append(start(copies.new(matched.at[0, group], matched.at[1, group], partner)))

    @pl.loop(0, 2)
    def _(g):
        match(g)

    pl.semaphore_wait(barrier, len(peers))
    send_cells(pl.ds(0, 2 * GROUP))
    tables_in = [
        start(copies.new(slots_i.at[0], slots_i.at[1], partner)),
        start(copies.new(slots_f.at[0], slots_f.at[1], partner)),
    ]
    depth_in = [start(copies.new(meta.at[k], meta_z.at[k], z_device(k))) for k in range(DEPTH - 1)]
    meta_z[DEPTH - 1] = meta[DEPTH - 1]
    for g in (2, 3):
        match(g)
        send_cells(pl.ds(g * GROUP, GROUP))

    for move in own_moves:
        move.wait()
    for copy in tables_in:
        copy.wait_recv()
    other_moves = [
        pltpu.make_async_copy(slots_i.at[1], table_i.at[1], move_sem.at[2]),
        pltpu.make_async_copy(slots_f.at[1], table_f.at[1], move_sem.at[3]),
    ]
    for move in other_moves:
        move.start()
    for move in other_moves:
        move.wait()
    for copy in cells_in:
        copy.wait_recv()

    across_at = (iota((PIX, PPIX), 1) - iota((PIX, PPIX), 0)).astype(F32).astype(BF16)
    down_at = (iota((PPIX, PIX), 0) - iota((PPIX, PIX), 1)).astype(F32).astype(BF16)

    def one_hot(at, offset, share):
        full = lambda value: jnp.full(at.shape, value, F32).astype(BF16)
        second = jnp.where(at == full(offset + 1.0), full(share), full(0.0))
        return jnp.where(at == full(offset), full(1.0 - share), second)

    count = len(CHUNKS)
    first = [sum(CHUNKS[:q]) for q in range(count)]
    refs = [chunk_refs[6 * q : 6 * q + 6] for q in range(count)]
    rings1, rings2, last = {}, {}, []

    def place(q, blocks):
        pieces = {}
        for i in range(CHUNKS[q]):
            z_to = lax.rem(z + distance_at(first[q] + i), DEPTH)
            for y_lo in range(2):
                slot = 2 * (z_to * 4 + y_lo * 2 + c)
                for source in range(2):
                    for r in range(2):
                        field = lambda f: table_f[source, f, slot + r]
                        across = one_hot(across_at, field(1), field(3))
                        wide = jnp.dot(
                            matched[source, table_i[source, 0, slot + r]],
                            across,
                            preferred_element_type=F32,
                        )
                        pieces[i, y_lo, source, r] = (field(4) * wide).astype(BF16)
        for i in range(CHUNKS[q]):
            z_to = lax.rem(z + distance_at(first[q] + i), DEPTH)
            for y_lo in range(2):
                slot = 2 * (z_to * 4 + y_lo * 2 + c)
                downs, placed = [], []
                for source in range(2):
                    for r in range(2):
                        field = lambda f: table_f[source, f, slot + r]
                        downs.append(one_hot(down_at, field(0), field(2)))
                        placed.append(pieces[i, y_lo, source, r])
                tile = jnp.dot(
                    jnp.concatenate(downs, axis=1),
                    jnp.concatenate(placed, axis=0),
                    preferred_element_type=F32,
                ).astype(BF16)
                for x_to in range(4):
                    for y_hi in range(2):
                        at = (x_to * 2 + y_hi) * ROWS
                        y_to = y_hi * 2 + y_lo
                        blocks[0, x_to, i, y_to] = tile[at : at + ROWS, :PIX]
                        blocks[1, y_to, i, x_to] = tile[at : at + ROWS, PIX:]

    def enter(q):
        blocks, relay, fin = refs[q][:3]
        place(q, blocks)
        for half in range(2):
            me, device = ((x, x_device), (y, y_device))[half]
            ring = Ring(copies, me, device, blocks.at[half], relay.at[half], fin.at[half])
            ring.start()
            rings1[q, half] = ring

    def forward(q):
        for half in range(2):
            rings1[q, half].forward()

    def turn(q):
        blocks, fin, relay = refs[q][3:6]
        for half in range(2):
            ring = rings1[q, half]
            ring.finish()
            for i in range(CHUNKS[q]):
                block = ring.result(i).astype(BF16)
                for other in range(4):
                    blocks[half, other, i] = block[other]
            me, device = ((y, y_device), (x, x_device))[half]
            if q < RING_PARTS:
                ring = Ring(copies, me, device, blocks.at[half], relay.at[half], fin.at[half])
            else:
                ring = Exchange(copies, me, device, blocks.at[half], fin.at[half])
            rings2[q, half] = ring
            rings2[q, half].start()

    def forward_second(q):
        for half in range(2):
            rings2[q, half].forward()

    def leave(q):
        for half in range(2):
            ring = rings2[q, half]
            ring.finish()
            for i in range(CHUNKS[q]):
                k = first[q] + i
                to = far_out if k < DEPTH - 1 else far_in
                to[k, half] = ring.result(i).astype(BF16)
        for i in range(CHUNKS[q]):
            k = first[q] + i
            if k < DEPTH - 1:
                last.append(start(copies.new(far_out.at[k], far_in.at[k], z_device(k))))

    def meta_first():
        for copy in depth_in:
            copy.wait_recv()
        total = meta_z[0]
        for k in range(1, DEPTH):
            total = total + meta_z[k]
        meta_x[x] = total
        return [
            start(copies.new(meta_x.at[x], meta_x.at[x], x_device((x + d) % 4))) for d in (1, 2, 3)
        ]

    def meta_second(before):
        for copy in before:
            copy.wait_recv()
        meta_y[y] = meta_x[...]
        return [
            start(copies.new(meta_y.at[y], meta_y.at[y], y_device((y + d) % 4))) for d in (1, 2, 3)
        ]

    def meta_third(before):
        for copy in before:
            copy.wait_recv()
        return start(copies.new(meta_y, meta_c, partner))

    enter(0)
    enter(1)
    forward(0)
    enter(2)
    sent_x = meta_first()
    forward(1)
    turn(0)
    enter(3)
    sent_y = meta_second(sent_x)
    forward(2)
    forward_second(0)
    turn(1)
    enter(4)
    leave(0)
    sent_c = meta_third(sent_y)
    forward(3)
    forward_second(1)
    turn(2)
    leave(1)
    forward(4)
    forward_second(2)
    turn(3)
    leave(2)

    sent_c.wait_recv()
    combo = (y % 2) * 2 + c
    mine = (iota((8, PIX), 1) // 2) % 4 == combo
    row_at = (iota((ROWS, PIX), 0) + (x * 2 + y // 2) * ROWS).astype(F32)
    column_at = iota((PPIX, PIX), 0).astype(F32)

    def cover(at, offset, share):
        rest = (1.0 - share).astype(BF16).astype(F32)
        d = at - offset
        once = jnp.where((d >= 0.0) & (d < float(PIX)), rest, 0.0)
        return once + jnp.where((d >= 1.0) & (d < float(PIX + 1)), share, 0.0)

    weight = jnp.zeros((ROWS, PPIX), F32)
    for source in (meta_y, meta_c):
        for b in range(4):
            full = jnp.zeros((8, PIX), F32)
            for m in range(4):
                kept = jnp.where(mine, source[b, m], 0.0)
                full = full + pltpu.roll(kept, lax.rem(2 * (m - combo) + PIX, PIX), 1)
            there = full[5:6] > 0.0
            inverse = jnp.where(there, 1.0 / jnp.where(there, full[4:5], 1.0), 0.0)
            down = inverse * cover(row_at, full[0:1], full[2:3])
            across = cover(column_at, full[1:2], full[3:4])
            weight = weight + lax.dot_general(
                down, across, (((1,), (1,)), ((), ())),
                precision=lax.Precision.HIGHEST, preferred_element_type=F32,
            )

    turn(4)
    leave(3)
    leave(4)
    for copy in last:
        copy.wait_recv()
    for half in range(2):
        total = far_in[0, half].astype(F32)
        for k in range(1, DEPTH):
            total = total + far_in[k, half].astype(F32)
        columns = slice(half * PIX, (half + 1) * PIX)
        out[:, columns] = total / jnp.sqrt(weight[:, columns] + 1.0)

    for copy in sent:
        copy.wait_send()
    for ring in list(rings1.values()) + list(rings2.values()):
        ring.drain()


COPY_COUNT = 3 + 2 + (DEPTH - 1) * 2 + 7 + len(CHUNKS) * 24


def chunk_shapes(n):
    return [
        pltpu.VMEM((2, 4, n, 4, ROWS, PIX), BF16),
        pltpu.VMEM((2, 2, n // 2, 4, ROWS, PIX), BF16),
        pltpu.VMEM((2, 2, n, 4, ROWS, PIX), BF16),
        pltpu.VMEM((2, 4, n, ROWS, PIX), BF16),
        pltpu.VMEM((2, 3, n, ROWS, PIX), BF16),
        pltpu.VMEM((2, 2, n // 2, ROWS, PIX), BF16),
    ]


def body(images, intersection, offsets, subpixel, variance, basis_index, coefficients):
    smem = pl.BlockSpec(memory_space=pltpu.SMEM)
    vmem = pl.BlockSpec(memory_space=pltpu.VMEM)
    scratch = [
        pltpu.VMEM((2, CELLS, PIX, PIX), BF16),
        pltpu.VMEM((2, 8, PIX), I32),
        pltpu.VMEM((2, 8, PIX), F32),
        pltpu.SMEM((2, 8, PIX), I32),
        pltpu.SMEM((2, 8, PIX), F32),
        pltpu.VMEM((DEPTH, 8, PIX), F32),
        pltpu.VMEM((DEPTH - 1, 2, ROWS, PIX), BF16),
        pltpu.VMEM((DEPTH, 2, ROWS, PIX), BF16),
        pltpu.VMEM((DEPTH, 8, PIX), F32),
        pltpu.VMEM((4, 8, PIX), F32),
        pltpu.VMEM((4, 4, 8, PIX), F32),
        pltpu.VMEM((4, 4, 8, PIX), F32),
        pltpu.SemaphoreType.DMA((COPY_COUNT,)),
        pltpu.SemaphoreType.DMA((COPY_COUNT,)),
        pltpu.SemaphoreType.DMA((4,)),
    ]
    for n in CHUNKS:
        scratch += chunk_shapes(n)
    out = pl.pallas_call(
        coadd_kernel,
        out_shape=jax.ShapeDtypeStruct((ROWS, PPIX), F32),
        in_specs=[smem] * 2 + [vmem] * 5,
        out_specs=vmem,
        scratch_shapes=scratch,
        compiler_params=pltpu.CompilerParams(
            collective_id=0, has_side_effects=True, vmem_limit_bytes=VMEM_LIMIT
        ),
    )(
        basis_index,
        jnp.transpose(coefficients, (1, 2, 0)),
        images[0],
        intersection[0].T,
        jnp.transpose(offsets[0], (1, 2, 0)),
        jnp.transpose(subpixel[0], (1, 2, 0)),
        variance,
    )
    return out[None]


def solution(mesh):
    return jax.shard_map(
        body,
        mesh=mesh,
        in_specs=(
            P("visit", "patch", None, None),
            P("visit", "patch", None),
            P("visit", "patch", None, None),
            P("visit", "patch", None, None),
            P("visit", "patch"),
            P("visit", "patch"),
            P(),
        ),
        out_specs=P("patch", "visit", None),
        check_vma=False,
    )
```
